128 devices in a mesh: pa: 32 (over y, x, core), mu: 4 (over z).
Axes of the slice: x: 4, y: 4, z: 4, core: 2. Of those that a mesh axis runs over, the one named last changes fastest.
Arguments:
- three_center: bfloat16 [4096, 256, 512], P('pa', 'mu'), may hold values from -6 to 6
- center_mask: int32 [64, 4, 8], P('pa', 'mu'), may hold values 0 or 1
- density: bfloat16 [512, 512], P('mu'), may hold values from -0.25 to 0.25
- density_mask: int32 [8, 8], P('mu'), may hold values 0 or 1
- metric_band: bfloat16 [4096, 384], P('pa'), may hold values from -0.3125 to 0.3125
Outputs:
- fitted: bfloat16 [4096, 256, 512], P('pa', 'mu')
- exchange_blocks: float32 [256, 64], P('mu')
The draws below stay inside these ranges and needn't reach their ends.
All inputs are finite; a program needn't handle non-finite values. No bound on the sum of `center_mask` or of `density_mask` on one device may be relied on, other than what follows from the above.
Results may differ from the reference program's by a relative error of at most 0.0051.
Values may be sent and summed in bfloat16 or wider, within the bound.
No kernel may reach another device: no remote copies, remote signals or barrier semaphores. Data moves between devices by JAX's collectives and lax.ppermute only.
A program may use at most 192 MiB of HBM per device.

```python
import math
import jax
import jax.numpy as jnp
from jax import lax

BS = 64
P_DEV = 128
MU_DEV = 64
NB = 512
NP = 4096
NMU = 256
N_PA = 32
N_MU = 4


def plant(entries, rng, low, top_value):
    longest = entries.shape.index(max(entries.shape))
    spots = []
    for shift in (0, 1):
        where = [jax.random.randint(jax.random.fold_in(rng, axis), (), 0, length) for axis, length in enumerate(entries.shape)]
        where[longest] = (where[longest] + shift) % entries.shape[longest]
        spots.append(tuple(where))
    return entries.at[spots[0]].set(low).at[spots[1]].set(top_value)


def steps_of(key, extent, shards, low, largest):
    def one(dim, blocks):
        draws = jax.random.uniform(jax.random.fold_in(jax.random.fold_in(key, 6), dim), (blocks,), jnp.float32, low / len(shards), largest / len(shards))
        return jnp.repeat(jnp.exp(draws), extent[dim] // blocks).reshape((-1,) + (1,) * (len(extent) - dim - 1))

    factor_of = one(*shards[0])
    for cut in shards[1:]:
        factor_of = factor_of * one(*cut)
    return factor_of


def gaussian(rng, shape, width, bound, cuts=(), kind=jnp.bfloat16):
    array = width * jax.random.normal(rng, shape, jnp.float32)
    if cuts:
        array = array * steps_of(rng, shape, cuts, -0.22, 0.18)
    return jnp.clip(array, -bound, bound).astype(kind)


def setup_inputs(seed: int = 0) -> dict:
    key_list = jax.random.split(jax.random.key(seed), 6)
    three_center = gaussian(key_list[0], (NP, NMU, NB), 1.0, 6.0, ((0, 32), (1, 4)))
    center_mask = plant((jax.random.randint(key_list[1], (NP // BS, NMU // BS, NB // BS), 0, 4) < 3).astype(jnp.int32), jax.random.fold_in(key_list[1], 1), 0, 1)
    density = gaussian(key_list[2], (NB, NB), NB ** -0.5, 0.25, ((0, 4),))
    density_mask = plant((jax.random.randint(key_list[3], (NB // BS, NB // BS), 0, 4) < 3).astype(jnp.int32), jax.random.fold_in(key_list[3], 1), 0, 1)
    metric_band = gaussian(key_list[4], (NP, 3 * P_DEV), (3 * P_DEV) ** -0.5, 0.3125, ((0, 32),))
    return {"three_center": three_center, "center_mask": center_mask, "density": density, "density_mask": density_mask, "metric_band": metric_band}


def reference(three_center, center_mask, density, density_mask, metric_band):
    blocks = three_center.reshape(NP // BS, BS, NMU // BS, BS, NB // BS, BS)
    weights = center_mask.astype(jnp.bfloat16)[:, None, :, None, :, None]
    masked = (blocks * weights).reshape(NP, NMU, NB)
    dens = (density.reshape(NB // BS, BS, NB // BS, BS) * density_mask.astype(jnp.bfloat16)[:, None, :, None]).reshape(NB, NB)
    half = jnp.dot(masked.reshape(NP * NMU, NB), dens, preferred_element_type=jnp.float32).astype(jnp.bfloat16).reshape(NP, NMU, NB)
    zeros = jnp.zeros((P_DEV, NMU, NB), jnp.bfloat16)
    padded = jnp.concatenate([zeros, half, zeros], axis=0)

    def one_range(index):
        start = (index * P_DEV).astype(jnp.int32)
        window = lax.dynamic_slice_in_dim(padded, start, 3 * P_DEV, 0)
        rows = lax.dynamic_slice_in_dim(metric_band, start, P_DEV, 0)
        return jnp.dot(rows, window.reshape(3 * P_DEV, NMU * NB), preferred_element_type=jnp.float32).astype(jnp.bfloat16)
    fitted = lax.map(one_range, jnp.arange(N_PA, dtype=jnp.int32)).reshape(NP, NMU, NB)
    scale = 1.0 / math.sqrt(NP * NB)
    pieces = []
    for block in range(N_MU):
        left = fitted[:, block * MU_DEV:(block + 1) * MU_DEV, :]
        right = masked[:, block * MU_DEV:(block + 1) * MU_DEV, :]
        pieces.append(lax.dot_general(left, right, (((0, 2), (0, 2)), ((), ())), preferred_element_type=jnp.float32) * scale)
    return (fitted, jnp.concatenate(pieces, axis=0))
```

```python
import math

import jax
import jax.numpy as jnp
from jax import lax
from jax.experimental import pallas as pl
from jax.experimental.pallas import tpu as pltpu
from jax.sharding import PartitionSpec as P

BS = 64
SIG = 128
PB = 16
QB = 8

CHUNKS = ((0, 0, 64), (128, 0, 64), (256, 0, 64), (384, 0, 32), (384, 32, 16), (384, 48, 16))
HALF_CALLS = ((0,), (1, 2, 3, 4, 5))


def half_kernel(chunks, s0, mask_ref, tc_ref, dens_ref, *refs):
    outs, scratch = refs[:-1], refs[-1]
    step = pl.program_id(0)
    cols = tc_ref.shape[1]
    mask = mask_ref[pl.ds((step * PB) // BS, 1), :]
    x = tc_ref[...].reshape(PB * cols, tc_ref.shape[2]) * mask.astype(jnp.bfloat16)
    flat = jnp.dot(x, dens_ref[...], preferred_element_type=jnp.float32)
    for t in range(scratch.shape[0]):
        scratch[t] = flat[:, t * SIG:(t + 1) * SIG]
    for out, (s, mu0, count) in zip(outs, chunks):
        for m in range(count):
            out[m] = scratch[(s - s0) // SIG, pl.ds(mu0 + m, PB, stride=cols), :].astype(jnp.bfloat16)


def half_call(tc, mask, dens, chunks):
    rows, cols, width = tc.shape
    s0 = min(s for s, _, _ in chunks)
    s1 = max(s for s, _, _ in chunks) + SIG
    return pl.pallas_call(
        lambda *refs: half_kernel(chunks, s0, *refs),
        grid=(rows // PB,),
        in_specs=[
            pl.BlockSpec(mask.shape, lambda i: (0, 0)),
            pl.BlockSpec((PB, cols, width), lambda i: (i, 0, 0)),
            pl.BlockSpec((width, s1 - s0), lambda i: (0, s0 // (s1 - s0))),
        ] if s0 % (s1 - s0) == 0 else [
            pl.BlockSpec(mask.shape, lambda i: (0, 0)),
            pl.BlockSpec((PB, cols, width), lambda i: (i, 0, 0)),
            pl.BlockSpec((width, s1 - s0), lambda i: (0, 0)),
        ],
        out_specs=[pl.BlockSpec((n, PB, SIG), lambda i: (0, i, 0)) for _, _, n in chunks],
        out_shape=[jax.ShapeDtypeStruct((n, rows, SIG), jnp.bfloat16) for _, _, n in chunks],
        scratch_shapes=[pltpu.VMEM(((s1 - s0) // SIG, PB * cols, SIG), jnp.float32)],
        compiler_params=pltpu.CompilerParams(vmem_limit_bytes=32 * 2**20),
        cost_estimate=pl.CostEstimate(
            flops=2 * rows * cols * width * (s1 - s0),
            bytes_accessed=2 * rows * cols * (width + s1 - s0),
            transcendentals=0,
        ),
    )(mask, tc, dens if s0 % (s1 - s0) == 0 else dens[:, s0:s1])


def fit_kernel(mu0, low_ref, own_ref, high_ref, metric_ref, tc_ref, mask_ref, acc_ref, *refs):
    fitted_ref, exch_ref, scratch = refs[-3:]
    count, rows, _ = own_ref.shape
    metric = metric_ref[...]

    def fit(pair, carry):
        columns = []
        for m in (2 * pair, 2 * pair + 1):
            columns.append(jnp.concatenate([low_ref[m], own_ref[m], high_ref[m]], axis=0))
        y = jnp.dot(metric, jnp.concatenate(columns, axis=1), preferred_element_type=jnp.float32)
        scratch[pl.ds(2 * pair, rows, stride=count), :] = y[:, :SIG]
        scratch[pl.ds(2 * pair + 1, rows, stride=count), :] = y[:, SIG:]
        return carry

    lax.fori_loop(0, count // 2, fit, 0, unroll=4)

    def contract(step, total):
        f = scratch[pl.ds(pl.multiple_of(step * QB * count, QB * count), QB * count), :]
        f = f.astype(jnp.bfloat16)
        first = pl.multiple_of(step * QB, QB)
        fitted_ref[pl.ds(first, QB)] = f.reshape(QB, count, SIG)
        g = f * mask_ref[pl.ds((step * QB) // BS, 1), :].astype(jnp.bfloat16)
        left = jnp.concatenate([g[q * count:(q + 1) * count] for q in range(QB)], axis=1)
        right = jnp.concatenate([tc_ref[first + q] for q in range(QB)], axis=1)
        return total + lax.dot_general(
            left, right, (((1,), (1,)), ((), ())), preferred_element_type=jnp.float32
        )

    total = lax.fori_loop(
        0, rows // QB, contract, jnp.zeros((count, tc_ref.shape[1]), jnp.float32), unroll=2
    )
    exch_ref[...] = acc_ref[...]
    exch_ref[mu0:mu0 + count, :] = acc_ref[mu0:mu0 + count, :] + total


def fit_call(chunk, low, own, high, metric, tc, mask, acc, fitted):
    s, mu0, count = chunk
    rows, cols, width = tc.shape
    block = pl.BlockSpec((count, rows, SIG), lambda i: (0, 0, 0))
    args = [low, own, high, metric, tc, mask, acc]
    in_specs = [
        block,
        block,
        block,
        pl.BlockSpec(metric.shape, lambda i: (0, 0)),
        pl.BlockSpec((rows, cols, SIG), lambda i: (0, 0, s // SIG)),
        pl.BlockSpec((mask.shape[0], SIG), lambda i: (0, s // SIG)),
        pl.BlockSpec(acc.shape, lambda i: (0, 0)),
    ]
    aliases = {}
    if fitted is not None:
        aliases = {len(args): 0}
        args.append(fitted)
        in_specs.append(pl.BlockSpec(memory_space=pl.ANY))
    return pl.pallas_call(
        lambda *refs: fit_kernel(mu0, *refs),
        grid=(1,),
        in_specs=in_specs,
        out_specs=[
            pl.BlockSpec((rows, count, SIG), lambda i: (0, mu0 // count, s // SIG)),
            pl.BlockSpec(acc.shape, lambda i: (0, 0)),
        ],
        out_shape=[
            jax.ShapeDtypeStruct(tc.shape, jnp.bfloat16),
            jax.ShapeDtypeStruct(acc.shape, jnp.float32),
        ],
        scratch_shapes=[pltpu.VMEM((rows * count, SIG), jnp.float32)],
        input_output_aliases=aliases,
        compiler_params=pltpu.CompilerParams(vmem_limit_bytes=40 * 2**20),
        cost_estimate=pl.CostEstimate(
            flops=2 * rows * count * SIG * (3 * rows + cols),
            bytes_accessed=2 * rows * SIG * (4 * count + cols),
            transcendentals=0,
        ),
    )(*args)


def gather_mu(local):
    count = lax.axis_size("mu")
    me = lax.axis_index("mu")
    parts = [local]
    for k in range(1, count):
        parts.append(lax.ppermute(local, "mu", [((i + k) % count, i) for i in range(count)]))
    twice = jnp.concatenate(parts + parts, axis=0)
    rows = local.shape[0]
    return lax.dynamic_slice_in_dim(twice, ((count - me) % count) * rows, count * rows, 0)


def rotate(value, stride, count, k):
    size = lax.axis_size("pa")
    span = stride * count
    pairs = [
        (i, (i // span) * span + ((i // stride + k) % count) * stride + i % stride)
        for i in range(size)
    ]
    return lax.ppermute(value, "pa", pairs)


def sum_pa(value):
    value = value + rotate(value, 1, 2, 1)
    for stride in (2, 8):
        parts = [rotate(value, stride, 4, k) for k in (1, 2, 3)]
        value = (value + parts[1]) + (parts[0] + parts[2])
    return value


def on_device(three_center, center_mask, density, density_mask, metric_band):
    rows, cols, width = three_center.shape
    drows = density.shape[0]
    block_mask = jnp.repeat(jnp.repeat(density_mask, BS, axis=0), BS, axis=1)
    dens = gather_mu(density * block_mask.astype(jnp.bfloat16))
    mask = jnp.repeat(center_mask[:, 0, :], BS, axis=1).astype(jnp.float32)

    count = lax.axis_size("pa")
    forward = [(i, i + 1) for i in range(count - 1)]
    backward = [(b, a) for a, b in forward]
    own = {}
    for call in HALF_CALLS:
        chunks = [CHUNKS[c] for c in call]
        for c, piece in zip(call, half_call(three_center, mask, dens, chunks)):
            own[c] = piece
    low = {c: lax.ppermute(own[c], "pa", forward) for c in own}
    high = {c: lax.ppermute(own[c], "pa", backward) for c in own}

    acc = jnp.zeros((cols, cols), jnp.float32)
    fitted = None
    for c, chunk in enumerate(CHUNKS):
        fitted, acc = fit_call(
            chunk, low[c], own[c], high[c], metric_band, three_center, mask, acc, fitted
        )
    scale = 1.0 / math.sqrt(rows * count * width)
    return (fitted, sum_pa(acc) * scale)


def solution(mesh):
    placed = (P("pa", "mu", None), P("pa", "mu", None), P("mu", None), P("mu", None), P("pa", None))
    return jax.shard_map(
        on_device,
        mesh=mesh,
        in_specs=placed,
        out_specs=(P("pa", "mu", None), P("mu", None)),
        check_vma=False,
    )
```

```python
import math

import jax
import jax.numpy as jnp
from jax import lax
from jax.experimental import pallas as pl
from jax.experimental.pallas import tpu as pltpu
from jax.sharding import PartitionSpec as P

BS = 64
SIG = 128
PB = 16
QB = 16
VMEM_BYTES = 56 * 2**20

RAW = (0, 4, 48, 16)
CHUNKS = ((0, 1, 0, 48), (128, 1, 0, 48), (256, 1, 0, 48), (384, 1, 0, 32), (384, 1, 32, 16))


def half_kernel(chunks, mu0, cols, mask_ref, tc_ref, dens_ref, *refs):
    outs, scratch = refs[:-1], refs[-1]
    x = tc_ref[...].reshape(PB * cols, tc_ref.shape[2])
    if mask_ref is not None:
        mask = mask_ref[pl.ds((pl.program_id(0) * PB) // BS, 1), :]
        x = x * mask.astype(jnp.bfloat16)
    flat = jnp.dot(x, dens_ref[...], preferred_element_type=jnp.float32)
    s0 = min(s for s, _, _, _ in chunks)
    pitch = cols + 1
    for t in range(scratch.shape[0]):
        for p in range(PB):
            scratch[t, p * pitch:p * pitch + cols] = flat[
                p * cols:(p + 1) * cols, t * SIG:(t + 1) * SIG
            ]
    for out, (s, tiles, first, count) in zip(outs, chunks):
        for t in range(tiles):
            for m in range(count):
                out[m, :, t * SIG:(t + 1) * SIG] = scratch[
                    (s - s0) // SIG + t, pl.ds(first - mu0 + m, PB, stride=pitch), :
                ].astype(jnp.bfloat16)


def half_call(tc, mask, dens, chunks, mu0, cols):
    rows, _, width = tc.shape
    s0 = min(s for s, _, _, _ in chunks)
    s1 = max(s + t * SIG for s, t, _, _ in chunks)
    args = [tc, dens[:, s0:s1]]
    in_specs = [
        pl.BlockSpec((PB, cols, width), lambda i: (i, 0, 0)),
        pl.BlockSpec((width, s1 - s0), lambda i: (0, 0)),
    ]
    if mask is not None:
        args.insert(0, mask)
        in_specs.insert(0, pl.BlockSpec(mask.shape, lambda i: (0, 0)))

    def kernel(*refs):
        half_kernel(chunks, mu0, cols, *(refs if mask is not None else (None,) + refs))

    return pl.pallas_call(
        kernel,
        grid=(rows // PB,),
        in_specs=in_specs,
        out_specs=[pl.BlockSpec((n, PB, t * SIG), lambda i: (0, i, 0)) for _, t, _, n in chunks],
        out_shape=[
            jax.ShapeDtypeStruct((n, rows, t * SIG), jnp.bfloat16) for _, t, _, n in chunks
        ],
        scratch_shapes=[
            pltpu.VMEM(((s1 - s0) // SIG, PB * (cols + 1) + 8, SIG), jnp.float32)
        ],
        compiler_params=pltpu.CompilerParams(vmem_limit_bytes=VMEM_BYTES),
        cost_estimate=pl.CostEstimate(
            flops=2 * rows * cols * width * (s1 - s0),
            bytes_accessed=2 * rows * cols * (width + s1 - s0),
            transcendentals=0,
        ),
    )(*args)


def fit_kernel(mu0, low_ref, own_ref, high_ref, metric_ref, tc_ref, mask_ref, acc_ref, *refs):
    fitted_ref, exch_ref, scratch = refs[-3:]
    count, rows, _ = own_ref.shape
    pitch = count + 1
    metric = metric_ref[...]

    def fit(pair, carry):
        columns = []
        for m in (2 * pair, 2 * pair + 1):
            columns.append(jnp.concatenate([low_ref[m], own_ref[m], high_ref[m]], axis=0))
        y = jnp.dot(metric, jnp.concatenate(columns, axis=1), preferred_element_type=jnp.float32)
        scratch[pl.ds(2 * pair, rows, stride=pitch), :] = y[:, :SIG]
        scratch[pl.ds(2 * pair + 1, rows, stride=pitch), :] = y[:, SIG:]
        return carry

    lax.fori_loop(0, count // 2, fit, 0, unroll=4)

    def contract(step, total):
        first = pl.multiple_of(step * QB, QB)
        fs = []
        for q in range(QB):
            fs.append(scratch[pl.ds((first + q) * pitch, count), :].astype(jnp.bfloat16))
            fitted_ref[first + q] = fs[-1]
        mask = mask_ref[pl.ds((step * QB) // BS, 1), :].astype(jnp.bfloat16)
        left = jnp.concatenate([f * mask for f in fs], axis=1)
        right = jnp.concatenate([tc_ref[first + q] for q in range(QB)], axis=1)
        return total + lax.dot_general(
            left, right, (((1,), (1,)), ((), ())), preferred_element_type=jnp.float32
        )

    total = lax.fori_loop(
        0, rows // QB, contract, jnp.zeros((count, tc_ref.shape[1]), jnp.float32), unroll=2
    )

    @pl.when(pl.program_id(0) == 0)
    def _():
        exch_ref[...] = acc_ref[...]

    exch_ref[mu0:mu0 + count, :] += total


def fit_call(chunk, low, own, high, metric, tc, mask, acc, fitted):
    s, tiles, mu0, count = chunk
    rows, cols, width = tc.shape
    block = pl.BlockSpec((count, rows, SIG), lambda i: (0, 0, i))
    args = [low, own, high, metric, tc, mask, acc]
    in_specs = [
        block,
        block,
        block,
        pl.BlockSpec(metric.shape, lambda i: (0, 0)),
        pl.BlockSpec((rows, cols, SIG), lambda i: (0, 0, s // SIG + i)),
        pl.BlockSpec((mask.shape[0], SIG), lambda i: (0, s // SIG + i)),
        pl.BlockSpec(acc.shape, lambda i: (0, 0)),
    ]
    aliases = {}
    if fitted is not None:
        aliases = {len(args): 0}
        args.append(fitted)
        in_specs.append(pl.BlockSpec(memory_space=pl.ANY))
    return pl.pallas_call(
        lambda *refs: fit_kernel(mu0, *refs),
        grid=(tiles,),
        in_specs=in_specs,
        out_specs=[
            pl.BlockSpec((rows, count, SIG), lambda i: (0, mu0 // count, s // SIG + i)),
            pl.BlockSpec(acc.shape, lambda i: (0, 0)),
        ],
        out_shape=[
            jax.ShapeDtypeStruct(tc.shape, jnp.bfloat16),
            jax.ShapeDtypeStruct(acc.shape, jnp.float32),
        ],
        scratch_shapes=[pltpu.VMEM((rows * (count + 1), SIG), jnp.float32)],
        input_output_aliases=aliases,
        compiler_params=pltpu.CompilerParams(vmem_limit_bytes=VMEM_BYTES),
        cost_estimate=pl.CostEstimate(
            flops=2 * rows * count * tiles * SIG * (3 * rows + cols),
            bytes_accessed=2 * rows * tiles * SIG * (4 * count + cols),
            transcendentals=0,
        ),
    )(*args)


def gather_mu(local):
    count = lax.axis_size("mu")
    me = lax.axis_index("mu")
    parts = [local]
    for k in range(1, count):
        parts.append(lax.ppermute(local, "mu", [((i + k) % count, i) for i in range(count)]))
    twice = jnp.concatenate(parts + parts, axis=0)
    rows = local.shape[0]
    return lax.dynamic_slice_in_dim(twice, ((count - me) % count) * rows, count * rows, 0)


def rotate(value, stride, count, k):
    size = lax.axis_size("pa")
    span = stride * count
    pairs = [
        (i, (i // span) * span + ((i // stride + k) % count) * stride + i % stride)
        for i in range(size)
    ]
    return lax.ppermute(value, "pa", pairs)


def sum_pa(value):
    value = value + rotate(value, 1, 2, 1)
    for stride in (2, 8):
        parts = [rotate(value, stride, 4, k) for k in (1, 2, 3)]
        value = (value + parts[1]) + (parts[0] + parts[2])
    return value


def on_device(three_center, center_mask, density, density_mask, metric_band):
    rows, cols, width = three_center.shape
    size = lax.axis_size("pa")
    forward = [(i, i + 1) for i in range(size - 1)]
    backward = [(b, a) for a, b in forward]

    mask = jnp.repeat(center_mask[:, 0, :], BS, axis=1).astype(jnp.float32)
    s, tiles, mu0, count = RAW
    raw = three_center[:, mu0:mu0 + count, :].reshape(rows // BS, BS, count, width)
    raw = (raw * mask.astype(jnp.bfloat16)[:, None, None, :]).reshape(rows, count, width)
    raw_low = lax.ppermute(raw, "pa", forward)
    raw_high = lax.ppermute(raw, "pa", backward)

    block_mask = jnp.repeat(jnp.repeat(density_mask, BS, axis=0), BS, axis=1)
    dens_local = density * block_mask.astype(jnp.bfloat16)
    dens = gather_mu(dens_local)

    own = list(half_call(three_center, mask, dens, CHUNKS[:1], 0, 48))
    *rest, own_raw = half_call(three_center, mask, dens, CHUNKS[1:] + (RAW,), 0, cols)
    own += rest

    def send(c, *after):
        piece, *_ = lax.optimization_barrier((own[c],) + after)
        return lax.ppermute(piece, "pa", forward), lax.ppermute(piece, "pa", backward)

    arrived = {0: send(0), 1: send(1)}
    (low,) = half_call(raw_low, None, dens, (RAW,), mu0, count)
    (high,) = half_call(raw_high, None, dens, (RAW,), mu0, count)
    acc = jnp.zeros((cols, cols), jnp.float32)
    fitted, acc = fit_call(RAW, low, own_raw, high, metric_band, three_center, mask, acc, None)
    arrived[2] = send(2, acc)
    for c, chunk in enumerate(CHUNKS):
        low, high = arrived[c]
        fitted, acc = fit_call(
            chunk, low, own[c], high, metric_band, three_center, mask, acc, fitted
        )
        if c + 3 < len(CHUNKS):
            arrived[c + 3] = send(c + 3, acc)
    scale = 1.0 / math.sqrt(rows * size * width)
    return (fitted, sum_pa(acc) * scale)


def solution(mesh):
    placed = (P("pa", "mu", None), P("pa", "mu", None), P("mu", None), P("mu", None), P("pa", None))
    return jax.shard_map(
        on_device,
        mesh=mesh,
        in_specs=placed,
        out_specs=(P("pa", "mu", None), P("mu", None)),
        check_vma=False,
    )
```

```python
import math

import jax
import jax.numpy as jnp
from jax import lax
from jax.experimental import pallas as pl
from jax.experimental.pallas import tpu as pltpu
from jax.sharding import PartitionSpec as P

BS = 64
SIG = 128
PB = 16
QB = 16
VMEM_BYTES = 56 * 2**20

RAW = (0, 4, 32, 32)
CHUNKS = ((0, 1, 0, 32), (128, 2, 0, 32), (384, 1, 0, 16), (384, 1, 16, 16))
WITH_RAW = (True, True, True, False)
ANY = pl.BlockSpec(memory_space=pl.ANY)
WHOLE = pl.BlockSpec(memory_space=pltpu.VMEM)
SCALE = 4.0
PARAMS = pltpu.CompilerParams(vmem_limit_bytes=VMEM_BYTES)


def cost(us):
    return pl.CostEstimate(
        flops=int(us * SCALE * 1e9), bytes_accessed=int(us * SCALE * 3.0e6), transcendentals=0
    )


def half_kernel(chunks, mu0, cols, mask_ref, dens_ref, tc_hbm, *refs):
    n = len(chunks)
    outs, staged = refs[:n], refs[n:2 * n]
    tc_buf, scratch, in_sem, out_sem = refs[2 * n:]
    blocks = tc_buf.shape[0] // PB
    s0 = min(s for s, _, _, _ in chunks)
    tiles_all = scratch.shape[0]
    pitch = cols + 1

    def fetch(b):
        rows = pl.ds(b * PB, PB)
        return pltpu.make_async_copy(
            tc_hbm.at[rows, pl.ds(0, cols)], tc_buf.at[rows], in_sem.at[b]
        )

    def put(k, b):
        return pltpu.make_async_copy(staged[k].at[:, b], outs[k].at[:, b], out_sem.at[k])

    for b in range(blocks):
        fetch(b).start()

    def step(b, carry):
        fetch(b).wait()
        x = tc_buf[pl.ds(b * PB, PB)].reshape(PB * cols, tc_buf.shape[2])
        if mask_ref is not None:
            x = x * mask_ref[(b * PB) // BS].astype(jnp.bfloat16)
        flat = jnp.dot(
            x, dens_ref[:, s0:s0 + tiles_all * SIG], preferred_element_type=jnp.float32
        )
        for t in range(tiles_all):
            for p in range(PB):
                scratch[t, p * pitch:p * pitch + cols] = flat[
                    p * cols:(p + 1) * cols, t * SIG:(t + 1) * SIG
                ]
        for k, (s, tiles, first, count) in enumerate(chunks):
            for t in range(tiles):
                for m in range(count):
                    staged[k][t, b, m] = scratch[
                        (s - s0) // SIG + t, pl.ds(first - mu0 + m, PB, stride=pitch), :
                    ].astype(jnp.bfloat16)
            put(k, b).start()
        return carry

    lax.fori_loop(0, blocks, step, 0)
    for k in range(n):
        pltpu.make_async_copy(staged[k], outs[k], out_sem.at[k]).wait()


def half_call(tc, mask, dens, chunks, mu0, cols):
    rows, _, width = tc.shape
    s0 = min(s for s, _, _, _ in chunks)
    s1 = max(s + t * SIG for s, t, _, _ in chunks)
    shapes = [(t, rows // PB, n, PB, SIG) for _, t, _, n in chunks]

    def kernel(*refs):
        half_kernel(chunks, mu0, cols, *(refs if mask is not None else (None,) + refs))

    return pl.pallas_call(
        kernel,
        in_specs=([WHOLE] if mask is not None else []) + [WHOLE, ANY],
        out_specs=[ANY] * len(chunks),
        out_shape=[jax.ShapeDtypeStruct(shape, jnp.bfloat16) for shape in shapes],
        scratch_shapes=[pltpu.VMEM(shape, jnp.bfloat16) for shape in shapes] + [
            pltpu.VMEM((rows, cols, width), jnp.bfloat16),
            pltpu.VMEM(((s1 - s0) // SIG, PB * (cols + 1) + 8, SIG), jnp.float32),
            pltpu.SemaphoreType.DMA((rows // PB,)),
            pltpu.SemaphoreType.DMA((len(chunks),)),
        ],
        compiler_params=PARAMS,
        cost_estimate=cost(6 if len(chunks) < 2 else 10),
    )(*([mask] if mask is not None else []), dens, tc)


def fit_tile(bufs, metric_ref, scratch, pitch):
    metric = metric_ref[...]
    rows = metric.shape[0]
    count = bufs[0].shape[1]

    def fit(pair, carry):
        columns = []
        for m in (2 * pair, 2 * pair + 1):
            columns.append(jnp.concatenate([r[:, m].reshape(rows, SIG) for r in bufs], axis=0))
        y = jnp.dot(metric, jnp.concatenate(columns, axis=1), preferred_element_type=jnp.float32)
        scratch[pl.ds(2 * pair, rows, stride=pitch), :] = y[:, :SIG]
        scratch[pl.ds(2 * pair + 1, rows, stride=pitch), :] = y[:, SIG:]
        return carry

    lax.fori_loop(0, count // 2, fit, 0, unroll=8)


def fit_raw_kernel(metric_ref, far, own, near, fitted, raw_rows, *refs):
    bufs, (staged, scratch, in_sem, out_sem) = refs[:3], refs[3:]
    s, tiles, mu0, count = RAW
    rows = metric_ref.shape[0]
    pitch = count + 1

    def fetch(t):
        return [
            pltpu.make_async_copy(src.at[t], buf.at[t], in_sem.at[k, t])
            for k, (src, buf) in enumerate(zip((far, own, near), bufs))
        ]

    def put(t):
        lanes = pl.ds(pl.multiple_of(s + t * SIG, SIG), SIG)
        return [
            pltpu.make_async_copy(
                staged.at[t], fitted.at[:, pl.ds(mu0, count), lanes], out_sem.at[0, t]
            ),
            pltpu.make_async_copy(staged.at[t], raw_rows.at[t], out_sem.at[1, t]),
        ]

    for t in range(tiles):
        for copy in fetch(t):
            copy.start()

    def tile(t, carry):
        for copy in fetch(t):
            copy.wait()
        fit_tile([buf.at[t] for buf in bufs], metric_ref, scratch, pitch)

        def store(step, inner):
            for q in range(QB):
                row = step * QB + q
                staged[t, row] = scratch[pl.ds(row * pitch, count), :].astype(jnp.bfloat16)
            return inner

        lax.fori_loop(0, rows // QB, store, 0)
        for copy in put(t):
            copy.start()
        return carry

    lax.fori_loop(0, tiles, tile, 0)
    for t in range(tiles):
        for copy in put(t):
            copy.wait()


def fit_raw_call(far, own, near, metric, shape):
    _, tiles, _, count = RAW
    rows = shape[0]
    buf = pltpu.VMEM((tiles, rows // PB, count, PB, SIG), jnp.bfloat16)
    return pl.pallas_call(
        fit_raw_kernel,
        in_specs=[WHOLE, ANY, ANY, ANY],
        out_specs=[ANY, ANY],
        out_shape=[
            jax.ShapeDtypeStruct(shape, jnp.bfloat16),
            jax.ShapeDtypeStruct((tiles, rows, count, SIG), jnp.bfloat16),
        ],
        scratch_shapes=[
            buf,
            buf,
            buf,
            pltpu.VMEM((tiles, rows, count, SIG), jnp.bfloat16),
            pltpu.VMEM((rows * (count + 1), SIG), jnp.float32),
            pltpu.SemaphoreType.DMA((3, tiles)),
            pltpu.SemaphoreType.DMA((2, tiles)),
        ],
        compiler_params=PARAMS,
        cost_estimate=cost(6),
    )(metric, far, own, near)


def fit_kernel(chunk, with_raw, metric_ref, mask_ref, acc_ref, far, own, near, tc, *refs):
    s, tiles, mu0, count = chunk
    raw, refs = (refs[0], refs[1:]) if with_raw else (None, refs)
    _, fitted, exch_ref, far_buf, own_buf, near_buf, tc_buf = refs[:7]
    raw_buf, refs = (refs[7], refs[8:]) if with_raw else (None, refs[7:])
    staged, scratch, in_sem, out_sem = refs
    rows = metric_ref.shape[0]
    pitch = count + 1
    lines = count + (RAW[3] if with_raw else 0)
    fit_bufs = (far_buf, own_buf, near_buf)

    def fetch(t):
        lanes = pl.ds(s + t * SIG, SIG)
        copies = [
            pltpu.make_async_copy(src.at[t], buf.at[t], in_sem.at[k, t])
            for k, (src, buf) in enumerate(zip((far, own, near), fit_bufs))
        ]
        copies.append(pltpu.make_async_copy(tc.at[:, :, lanes], tc_buf.at[t], in_sem.at[3, t]))
        if with_raw:
            copies.append(
                pltpu.make_async_copy(raw.at[s // SIG + t], raw_buf.at[t], in_sem.at[4, t])
            )
        return copies

    def put(t):
        lanes = pl.ds(s + t * SIG, SIG)
        return pltpu.make_async_copy(
            staged.at[t], fitted.at[:, pl.ds(mu0, count), lanes], out_sem.at[t]
        )

    for t in range(tiles):
        for copy in fetch(t):
            copy.start()
    exch_ref[...] = acc_ref[...]
    for t in range(tiles):
        copies = fetch(t)
        for copy in copies[:3]:
            copy.wait()
        fit_tile([buf.at[t] for buf in fit_bufs], metric_ref, scratch, pitch)
        for copy in copies[3:]:
            copy.wait()

        def contract(block, total, t=t):
            first = pl.multiple_of(block * QB, QB)
            mask = mask_ref[(block * QB) // BS, :, s + t * SIG:s + (t + 1) * SIG]
            mask = mask.astype(jnp.bfloat16)
            left = []
            for q in range(QB):
                f = scratch[pl.ds((first + q) * pitch, count), :].astype(jnp.bfloat16)
                staged[t, first + q] = f
                if with_raw:
                    f = jnp.concatenate([f, raw_buf[t, first + q]], axis=0)
                left.append(f * mask)
            right = [tc_buf[t, first + q] for q in range(QB)]
            return total + lax.dot_general(
                jnp.concatenate(left, axis=1),
                jnp.concatenate(right, axis=1),
                (((1,), (1,)), ((), ())),
                preferred_element_type=jnp.float32,
            )

        total = lax.fori_loop(
            0, rows // QB, contract, jnp.zeros((lines, acc_ref.shape[1]), jnp.float32), unroll=2
        )
        put(t).start()
        exch_ref[mu0:mu0 + count, :] += total[:count]
        if with_raw:
            exch_ref[RAW[2]:RAW[2] + RAW[3], :] += total[count:]
    for t in range(tiles):
        put(t).wait()


def fit_call(chunk, far, own, near, metric, tc, mask, acc, raw_rows, fitted):
    s, tiles, mu0, count = chunk
    rows, cols, width = tc.shape
    with_raw = raw_rows is not None
    args = [metric, mask, acc, far, own, near, tc] + ([raw_rows] if with_raw else []) + [fitted]
    buf = pltpu.VMEM((tiles, rows // PB, count, PB, SIG), jnp.bfloat16)
    return pl.pallas_call(
        lambda *refs: fit_kernel(chunk, with_raw, *refs),
        in_specs=[WHOLE] * 3 + [ANY] * (len(args) - 3),
        out_specs=[ANY, WHOLE],
        out_shape=[
            jax.ShapeDtypeStruct(tc.shape, jnp.bfloat16),
            jax.ShapeDtypeStruct(acc.shape, jnp.float32),
        ],
        scratch_shapes=[buf, buf, buf, pltpu.VMEM((tiles, rows, cols, SIG), jnp.bfloat16)]
        + ([pltpu.VMEM((tiles, rows, RAW[3], SIG), jnp.bfloat16)] if with_raw else [])
        + [
            pltpu.VMEM((tiles, rows, count, SIG), jnp.bfloat16),
            pltpu.VMEM((rows * (count + 1), SIG), jnp.float32),
            pltpu.SemaphoreType.DMA((5, tiles)),
            pltpu.SemaphoreType.DMA((tiles,)),
        ],
        input_output_aliases={len(args) - 1: 0},
        compiler_params=PARAMS,
        cost_estimate=cost(3 + tiles * count / 16),
    )(*args)


def gather_mu(local):
    count = lax.axis_size("mu")
    me = lax.axis_index("mu")
    parts = [local]
    for k in range(1, count):
        parts.append(lax.ppermute(local, "mu", [((i + k) % count, i) for i in range(count)]))
    twice = jnp.concatenate(parts + parts, axis=0)
    rows = local.shape[0]
    return lax.dynamic_slice_in_dim(twice, ((count - me) % count) * rows, count * rows, 0)


def rotate(value, stride, count, k):
    size = lax.axis_size("pa")
    span = stride * count
    pairs = [
        (i, (i // span) * span + ((i // stride + k) % count) * stride + i % stride)
        for i in range(size)
    ]
    return lax.ppermute(value, "pa", pairs)


def sum_pa(value):
    value = value + rotate(value, 1, 2, 1)
    for stride in (2, 8):
        parts = [rotate(value, stride, 4, k) for k in (1, 2, 3)]
        value = (value + parts[1]) + (parts[0] + parts[2])
    return value


def after(value, *earlier):
    return lax.optimization_barrier((value,) + earlier)[0]


def on_device(three_center, center_mask, density, density_mask, metric_band):
    rows, cols, width = three_center.shape
    size = lax.axis_size("pa")
    near_pairs = [(i, i ^ 1) for i in range(size)]
    far_pairs = [(i, i + 1 if i % 2 else i - 1) for i in range(1, size - 1)]

    def to_near(value, *earlier):
        return lax.ppermute(after(value, *earlier), "pa", near_pairs)

    def to_far(value, *earlier):
        return lax.ppermute(after(value, *earlier), "pa", far_pairs)

    mask = jnp.repeat(center_mask, BS, axis=2).astype(jnp.float32)
    _, _, mu0, count = RAW
    raw = three_center[:, mu0:mu0 + count, :].reshape(rows // BS, BS, count, width)
    raw = (raw * mask.astype(jnp.bfloat16)[:, None]).reshape(rows, count, width)
    raw_far = to_far(raw)

    block_mask = jnp.repeat(jnp.repeat(density_mask, BS, axis=0), BS, axis=1)
    dens = gather_mu(after(density * block_mask.astype(jnp.bfloat16), raw))
    low, middle, high = jnp.split(metric_band, 3, axis=1)
    metric = jnp.where(
        lax.axis_index("pa") % 2 == 0,
        metric_band,
        jnp.concatenate([high, middle, low], axis=1),
    )

    *own, own_raw = half_call(three_center, mask, dens, CHUNKS + (RAW,), 0, cols)
    far = [to_far(own[0]), to_far(own[1])]
    near_raw = to_near(own_raw)
    (half_far,) = half_call(raw_far, None, after(dens, own_raw), (RAW,), mu0, count)
    near = [to_near(own[0], half_far)]
    fitted, raw_rows = fit_raw_call(half_far, own_raw, near_raw, metric, three_center.shape)
    far.append(to_far(own[2], raw_rows))
    near.append(to_near(own[1], raw_rows))
    acc = jnp.zeros((cols, cols), jnp.float32)
    for c, chunk in enumerate(CHUNKS):
        fitted, acc = fit_call(
            chunk, far[c], own[c], near[c], metric, three_center, mask, acc,
            raw_rows if WITH_RAW[c] else None, fitted,
        )
        if c + 3 < len(CHUNKS):
            far.append(to_far(own[c + 3], acc))
        if c + 2 < len(CHUNKS):
            near.append(to_near(own[c + 2], acc))
    scale = 1.0 / math.sqrt(rows * size * width)
    return (fitted, sum_pa(acc) * scale)


def solution(mesh):
    placed = (P("pa", "mu", None), P("pa", "mu", None), P("mu", None), P("mu", None), P("pa", None))
    return jax.shard_map(
        on_device,
        mesh=mesh,
        in_specs=placed,
        out_specs=(P("pa", "mu", None), P("mu", None)),
        check_vma=False,
    )
```

```python
import math

import jax
import jax.numpy as jnp
from jax import lax
from jax.experimental import pallas as pl
from jax.experimental.pallas import tpu as pltpu
from jax.sharding import PartitionSpec as P

BS = 64
SIG = 128
PB = 16
QB = 16
MIB = 2**20

RAW_MU = 32
RAW_STEP = 32
CHUNKS = ((0, 0, 32), (128, 0, 32), (256, 0, 32), (384, 0, 16), (384, 16, 16))
WITH_RAW = (True, True, True, True, False)
HALF_MIB = 56
HALF_COST = 1
FIT_MIB = 24
FAR_COST = 20
FIT_COST = 0.3
ANY = pl.BlockSpec(memory_space=pl.ANY)
WHOLE = pl.BlockSpec(memory_space=pltpu.VMEM)


def cost(us):
    return pl.CostEstimate(
        flops=int(us * 4e9), bytes_accessed=int(us * 12e6), transcendentals=0
    )


def params(mib):
    return pltpu.CompilerParams(vmem_limit_bytes=mib * MIB)


def half_rows(x, dens, scratch, cols):
    flat = jnp.dot(x.reshape(PB * cols, x.shape[2]), dens, preferred_element_type=jnp.float32)
    pitch = cols + 1
    for t in range(scratch.shape[0]):
        for p in range(PB):
            scratch[t, p * pitch:p * pitch + cols] = flat[
                p * cols:(p + 1) * cols, t * SIG:(t + 1) * SIG
            ]


def turned(scratch, t, m, cols):
    return scratch[t, pl.ds(m, PB, stride=cols + 1), :].astype(jnp.bfloat16)


def half_kernel(mask_ref, *refs):
    parts, tc_hbm = refs[:4], refs[4]
    dens_ref, all_hbm, chunk_hbm = refs[5], refs[6], refs[7:-5]
    tc_buf, staged, scratch, in_sem, out_sem = refs[-5:]
    rows, cols, width = tc_buf.shape
    blocks = rows // PB

    def fetch(b):
        rows_b = pl.ds(b * PB, PB)
        return pltpu.make_async_copy(tc_hbm.at[rows_b], tc_buf.at[rows_b], in_sem.at[b])

    for b in range(blocks):
        fetch(b).start()
    me = lax.axis_index("mu")
    depth = parts[0].shape[0]
    for k, part in enumerate(parts):
        at = lax.rem(me + k, len(parts)) * depth
        dens_ref[pl.ds(pl.multiple_of(at, depth), depth), :] = part[...]

    def step(b, carry):
        fetch(b).wait()
        x = tc_buf[pl.ds(b * PB, PB)] * mask_ref[(b * PB) // BS].astype(jnp.bfloat16)
        half_rows(x, dens_ref[...], scratch, cols)
        for t in range(width // SIG):
            for m in range(cols):
                staged[t, b, m] = turned(scratch, t, m, cols)
        for k, (s, mu0, count) in enumerate(CHUNKS):
            part = staged.at[s // SIG, b, pl.ds(mu0, count)]
            pltpu.make_async_copy(part, chunk_hbm[k].at[b], out_sem.at[k]).start()
        pltpu.make_async_copy(staged.at[:, b], all_hbm.at[:, b], out_sem.at[len(CHUNKS)]).start()
        return carry

    lax.fori_loop(0, blocks, step, 0)
    for k, (s, mu0, count) in enumerate(CHUNKS):
        part = staged.at[s // SIG, :, pl.ds(mu0, count)]
        pltpu.make_async_copy(part, chunk_hbm[k], out_sem.at[k]).wait()
    pltpu.make_async_copy(staged, all_hbm, out_sem.at[len(CHUNKS)]).wait()


def half_call(tc, mask, parts):
    rows, cols, width = tc.shape
    whole = (width // SIG, rows // PB, cols, PB, SIG)
    shapes = [(width, width), whole] + [(rows // PB, n, PB, SIG) for _, _, n in CHUNKS]
    return pl.pallas_call(
        half_kernel,
        in_specs=[WHOLE] * (1 + len(parts)) + [ANY],
        out_specs=[WHOLE] + [ANY] * (len(CHUNKS) + 1),
        out_shape=[jax.ShapeDtypeStruct(shape, jnp.bfloat16) for shape in shapes],
        scratch_shapes=[
            pltpu.VMEM(tc.shape, jnp.bfloat16),
            pltpu.VMEM(whole, jnp.bfloat16),
            pltpu.VMEM((width // SIG, PB * (cols + 1) + 8, SIG), jnp.float32),
            pltpu.SemaphoreType.DMA((rows // PB,)),
            pltpu.SemaphoreType.DMA((len(CHUNKS) + 1,)),
        ],
        compiler_params=params(HALF_MIB),
        cost_estimate=cost(HALF_COST),
    )(mask, *parts, tc)


def far_half_kernel(dens_ref, raw_ref, out_ref, scratch):
    def step(b, carry):
        half_block(dens_ref, raw_ref, out_ref, scratch, b)
        return carry

    lax.fori_loop(0, raw_ref.shape[0] // PB, step, 0)


def half_block(dens_ref, raw_ref, out_ref, scratch, b):
    cols = raw_ref.shape[1]
    half_rows(raw_ref[pl.ds(b * PB, PB)], dens_ref[...], scratch, cols)
    for t in range(scratch.shape[0]):
        for m in range(cols):
            out_ref[t, b, m] = turned(scratch, t, m, cols)


def far_half_call(raw_far, dens):
    rows, count, width = raw_far.shape
    return pl.pallas_call(
        far_half_kernel,
        in_specs=[WHOLE, WHOLE],
        out_specs=WHOLE,
        out_shape=jax.ShapeDtypeStruct(
            (width // SIG, rows // PB, count, PB, SIG), jnp.bfloat16
        ),
        scratch_shapes=[pltpu.VMEM((width // SIG, PB * (count + 1) + 8, SIG), jnp.float32)],
        compiler_params=params(16),
        cost_estimate=cost(FAR_COST),
    )(dens, raw_far)


def fit_tile(pieces, metric_ref, scratch, pitch, count):
    metric = metric_ref[...]
    rows = metric.shape[0]

    def fit(pair, carry):
        columns = [jnp.concatenate(pieces(m), axis=0) for m in (2 * pair, 2 * pair + 1)]
        y = jnp.dot(metric, jnp.concatenate(columns, axis=1), preferred_element_type=jnp.float32)
        scratch[pl.ds(2 * pair, rows, stride=pitch), :] = y[:, :SIG]
        scratch[pl.ds(2 * pair + 1, rows, stride=pitch), :] = y[:, SIG:]
        return carry

    lax.fori_loop(0, count // 2, fit, 0, unroll=8)


def raw_kernel(metric_ref, far_ref, own, near, fitted, rows_ref, *refs):
    own_buf, near_buf, scratch, in_sem, out_sem = refs
    tiles, rows, count, _ = rows_ref.shape
    pitch = count + 1
    part = pl.ds(RAW_MU, count)

    def fetch(t):
        return [
            pltpu.make_async_copy(src.at[t, :, part], buf.at[t], in_sem.at[k, t])
            for k, (src, buf) in enumerate(((own, own_buf), (near, near_buf)))
        ]

    def put(t):
        lanes = pl.ds(pl.multiple_of(t * SIG, SIG), SIG)
        return pltpu.make_async_copy(rows_ref.at[t], fitted.at[:, part, lanes], out_sem.at[t])

    for t in range(tiles):
        for copy in fetch(t):
            copy.start()

    def tile(t, carry):
        for copy in fetch(t):
            copy.wait()

        def pieces(m):
            return [buf[t, :, m].reshape(rows, SIG) for buf in (far_ref, own_buf, near_buf)]

        fit_tile(pieces, metric_ref, scratch, pitch, count)

        def store(block, inner):
            for q in range(QB):
                row = block * QB + q
                rows_ref[t, row] = scratch[pl.ds(row * pitch, count), :].astype(jnp.bfloat16)
            return inner

        lax.fori_loop(0, rows // QB, store, 0)
        put(t).start()
        return carry

    lax.fori_loop(0, tiles, tile, 0)
    for t in range(tiles):
        put(t).wait()


def raw_call(far, own, near, metric, shape):
    rows, _, width = shape
    count = RAW_STEP
    tiles = width // SIG
    buf = pltpu.VMEM((tiles, rows // PB, count, PB, SIG), jnp.bfloat16)
    return pl.pallas_call(
        raw_kernel,
        in_specs=[WHOLE, WHOLE, ANY, ANY],
        out_specs=[ANY, WHOLE],
        out_shape=[
            jax.ShapeDtypeStruct(shape, jnp.bfloat16),
            jax.ShapeDtypeStruct((tiles, rows, count, SIG), jnp.bfloat16),
        ],
        scratch_shapes=[
            buf,
            buf,
            pltpu.VMEM((rows * (count + 1), SIG), jnp.float32),
            pltpu.SemaphoreType.DMA((2, tiles)),
            pltpu.SemaphoreType.DMA((tiles,)),
        ],
        compiler_params=params(FIT_MIB),
        cost_estimate=cost(FIT_COST),
    )(metric, far, own, near)


def fit_kernel(chunk, raws, metric_ref, mask_ref, acc_ref, far_ref, *refs):
    s, mu0, count = chunk
    raw_refs, refs = refs[:raws], refs[raws:]
    own, near, tc, _, fitted, exch_ref, own_buf, near_buf, tc_buf, staged, scratch = refs[:11]
    in_sem, out_sem = refs[11:]
    rows = metric_ref.shape[0]
    pitch = count + 1
    tile = s // SIG
    part = pl.ds(mu0, count)
    lanes = pl.ds(s, SIG)
    copies = [
        pltpu.make_async_copy(src, buf, in_sem.at[k])
        for k, (src, buf) in enumerate((
            (own.at[tile, :, part], own_buf),
            (near.at[tile, :, part], near_buf),
            (tc.at[:, :, lanes], tc_buf),
        ))
    ]
    for copy in copies:
        copy.start()
    for copy in copies[:2]:
        copy.wait()

    def pieces(m):
        return [buf[:, m].reshape(rows, SIG) for buf in (far_ref, own_buf, near_buf)]

    fit_tile(pieces, metric_ref, scratch, pitch, count)
    copies[2].wait()

    def contract(block, total):
        first = pl.multiple_of(block * QB, QB)
        mask = mask_ref[(block * QB) // BS, :, s:s + SIG].astype(jnp.bfloat16)
        left = []
        for q in range(QB):
            f = scratch[pl.ds((first + q) * pitch, count), :].astype(jnp.bfloat16)
            staged[first + q] = f
            if raws:
                f = jnp.concatenate([f] + [r[tile, first + q] for r in raw_refs], axis=0)
            left.append(f * mask)
        right = [tc_buf[first + q] for q in range(QB)]
        return total + lax.dot_general(
            jnp.concatenate(left, axis=1),
            jnp.concatenate(right, axis=1),
            (((1,), (1,)), ((), ())),
            preferred_element_type=jnp.float32,
        )

    lines = count + raws * RAW_STEP
    total = lax.fori_loop(
        0, rows // QB, contract, jnp.zeros((lines, acc_ref.shape[1]), jnp.float32), unroll=2
    )
    store = pltpu.make_async_copy(staged, fitted.at[:, part, lanes], out_sem)
    store.start()
    exch_ref[...] = acc_ref[...]
    exch_ref[mu0:mu0 + count, :] += total[:count]
    if raws:
        exch_ref[RAW_MU:, :] += total[count:]
    store.wait()


def fit_call(chunk, far, own, near, metric, tc, mask, acc, raw_rows, fitted):
    _, _, count = chunk
    rows, cols, _ = tc.shape
    raws = len(raw_rows)
    args = [metric, mask, acc, far, *raw_rows, own, near, tc, fitted]
    buf = pltpu.VMEM((rows // PB, count, PB, SIG), jnp.bfloat16)
    return pl.pallas_call(
        lambda *refs: fit_kernel(chunk, raws, *refs),
        in_specs=[WHOLE] * (4 + raws) + [ANY] * 4,
        out_specs=[ANY, WHOLE],
        out_shape=[
            jax.ShapeDtypeStruct(tc.shape, jnp.bfloat16),
            jax.ShapeDtypeStruct(acc.shape, jnp.float32),
        ],
        scratch_shapes=[
            buf,
            buf,
            pltpu.VMEM((rows, cols, SIG), jnp.bfloat16),
            pltpu.VMEM((rows, count, SIG), jnp.bfloat16),
            pltpu.VMEM((rows * (count + 1), SIG), jnp.float32),
            pltpu.SemaphoreType.DMA((3,)),
            pltpu.SemaphoreType.DMA,
        ],
        input_output_aliases={len(args) - 1: 0},
        compiler_params=params(FIT_MIB),
        cost_estimate=cost(FIT_COST),
    )(*args)


def rotate(value, stride, count, k):
    size = lax.axis_size("pa")
    span = stride * count
    pairs = [
        (i, (i // span) * span + ((i // stride + k) % count) * stride + i % stride)
        for i in range(size)
    ]
    return lax.ppermute(value, "pa", pairs)


def sum_pa(value):
    value = value + rotate(value, 1, 2, 1)
    for stride in (2, 8):
        parts = [rotate(value, stride, 4, k) for k in (1, 2, 3)]
        value = (value + parts[1]) + (parts[0] + parts[2])
    return value


def after(value, *earlier):
    return lax.optimization_barrier((value,) + earlier)[0]


def on_device(three_center, center_mask, density, density_mask, metric_band):
    rows, cols, width = three_center.shape
    size = lax.axis_size("pa")
    near_pairs = [(i, i ^ 1) for i in range(size)]
    far_pairs = [(i, i + 1 if i % 2 else i - 1) for i in range(1, size - 1)]

    def to_far(value, *earlier):
        return lax.ppermute(after(value, *earlier), "pa", far_pairs)

    mask = jnp.repeat(center_mask, BS, axis=2).astype(jnp.float32)

    def masked(mu0, lane_mask):
        piece = three_center[:, mu0:mu0 + RAW_STEP, :].reshape(rows // BS, BS, RAW_STEP, width)
        piece = piece * lane_mask.astype(jnp.bfloat16)[:, None]
        return piece.reshape(rows, RAW_STEP, width)

    raw = masked(RAW_MU, mask)
    raw_far = to_far(raw)
    block_mask = jnp.repeat(jnp.repeat(density_mask, BS, axis=0), BS, axis=1)
    local = after(density * block_mask.astype(jnp.bfloat16), raw)
    count = lax.axis_size("mu")
    parts = [local] + [
        lax.ppermute(local, "mu", [((i + k) % count, i) for i in range(count)])
        for k in range(1, count)
    ]
    low, middle, high = jnp.split(metric_band, 3, axis=1)
    metric = jnp.where(
        lax.axis_index("pa") % 2 == 0,
        metric_band,
        jnp.concatenate([high, middle, low], axis=1),
    )

    dens, own, *chunks = half_call(three_center, mask, parts)
    far = [to_far(chunks[0])]
    near = lax.ppermute(own, "pa", near_pairs)
    half_far = far_half_call(raw_far, dens)
    far.append(to_far(chunks[1], half_far))
    fitted, raw_rows = raw_call(half_far, own, near, metric, three_center.shape)
    far += [to_far(chunks[2], raw_rows), to_far(chunks[3], raw_rows)]
    acc = jnp.zeros((cols, cols), jnp.float32)
    for c, chunk in enumerate(CHUNKS):
        fitted, acc = fit_call(
            chunk, far[c], own, near, metric, three_center, mask, acc,
            [raw_rows] if WITH_RAW[c] else [], fitted,
        )
        if len(far) < len(CHUNKS):
            far.append(to_far(chunks[len(far)], acc))
    scale = 1.0 / math.sqrt(rows * size * width)
    return (fitted, sum_pa(acc) * scale)


def solution(mesh):
    placed = (P("pa", "mu", None), P("pa", "mu", None), P("mu", None), P("mu", None), P("pa", None))
    return jax.shard_map(
        on_device,
        mesh=mesh,
        in_specs=placed,
        out_specs=(P("pa", "mu", None), P("mu", None)),
        check_vma=False,
    )
```

```python
import math

import jax
import jax.numpy as jnp
from jax import lax
from jax.experimental import pallas as pl
from jax.experimental.pallas import tpu as pltpu
from jax.sharding import PartitionSpec as P

BS = 64
SIG = 128
PB = 16
QB = 16
MIB = 2**20

RAW_MU = 32
RAW_STEP = 32
LOW = (0, 4, 0, 32)
RAW_HALVES = ((0, 2, 32, 32), (256, 2, 32, 32))
CHUNKS = ((0, 2, 0, 32), (256, 1, 0, 32), (384, 1, 0, 16), (384, 1, 16, 16))
PIECES = (LOW,) + RAW_HALVES + CHUNKS
HALF_MIB = 56
HALF_COST = 1
FIT_MIB = 40
RAW_MIB = 32
FIT_COST = 0.3
HBM = pl.BlockSpec(memory_space=pltpu.HBM)
WHOLE = pl.BlockSpec(memory_space=pltpu.VMEM)


def cost(us):
    return pl.CostEstimate(
        flops=int(us * 4e9), bytes_accessed=int(us * 12e6), transcendentals=0
    )


def params(mib):
    return pltpu.CompilerParams(vmem_limit_bytes=mib * MIB)


def half_rows(x, dens, scratch, cols):
    flat = jnp.dot(x.reshape(PB * cols, x.shape[2]), dens, preferred_element_type=jnp.float32)
    pitch = cols + 1
    for t in range(scratch.shape[0]):
        for p in range(PB):
            scratch[t, p * pitch:p * pitch + cols] = flat[
                p * cols:(p + 1) * cols, t * SIG:(t + 1) * SIG
            ]


def turned(scratch, t, m, cols):
    return scratch[t, pl.ds(m, PB, stride=cols + 1), :].astype(jnp.bfloat16)


def half_kernel(mask_ref, *refs):
    parts, tc_hbm = refs[:4], refs[4]
    dens_ref, outs = refs[5], refs[6:-5]
    tc_buf, staged, scratch, in_sem, out_sem = refs[-5:]
    rows, cols, width = tc_buf.shape
    blocks = rows // PB

    def fetch(b):
        rows_b = pl.ds(b * PB, PB)
        return pltpu.make_async_copy(tc_hbm.at[rows_b], tc_buf.at[rows_b], in_sem.at[b])

    for b in range(blocks):
        fetch(b).start()
    me = lax.axis_index("mu")
    depth = parts[0].shape[0]
    for k, part in enumerate(parts):
        at = lax.rem(me + k, len(parts)) * depth
        dens_ref[pl.ds(pl.multiple_of(at, depth), depth), :] = part[...]

    def step(b, carry):
        fetch(b).wait()
        x = tc_buf[pl.ds(b * PB, PB)] * mask_ref[(b * PB) // BS].astype(jnp.bfloat16)
        half_rows(x, dens_ref[...], scratch, cols)
        for t in range(width // SIG):
            for m in range(cols):
                staged[t, b, m] = turned(scratch, t, m, cols)
        for k, (s, tiles, mu0, count) in enumerate(PIECES):
            part = staged.at[pl.ds(s // SIG, tiles), b, pl.ds(mu0, count)]
            pltpu.make_async_copy(part, outs[k].at[:, b], out_sem.at[k]).start()
        return carry

    lax.fori_loop(0, blocks, step, 0)
    for k, (s, tiles, mu0, count) in enumerate(PIECES):
        part = staged.at[pl.ds(s // SIG, tiles), :, pl.ds(mu0, count)]
        pltpu.make_async_copy(part, outs[k], out_sem.at[k]).wait()


def half_call(tc, mask, parts):
    rows, cols, width = tc.shape
    whole = (width // SIG, rows // PB, cols, PB, SIG)
    shapes = [(width, width)] + [(t, rows // PB, n, PB, SIG) for _, t, _, n in PIECES]
    return pl.pallas_call(
        half_kernel,
        in_specs=[WHOLE] * (1 + len(parts)) + [HBM],
        out_specs=[WHOLE] + [HBM] * len(PIECES),
        out_shape=[jax.ShapeDtypeStruct(shape, jnp.bfloat16) for shape in shapes],
        scratch_shapes=[
            pltpu.VMEM(tc.shape, jnp.bfloat16),
            pltpu.VMEM(whole, jnp.bfloat16),
            pltpu.VMEM((width // SIG, PB * (cols + 1) + 8, SIG), jnp.float32),
            pltpu.SemaphoreType.DMA((rows // PB,)),
            pltpu.SemaphoreType.DMA((len(PIECES),)),
        ],
        compiler_params=params(HALF_MIB),
        cost_estimate=cost(HALF_COST),
    )(mask, *parts, tc)


def raw_kernel_send(mask_ref, tc, out, bufs, in_sem, out_sem):
    rows, count, width = bufs.shape
    step = rows // in_sem.shape[0]

    def fetch(b):
        part = pl.ds(b * step, step)
        source = tc.at[part, pl.ds(RAW_MU, RAW_STEP)]
        return pltpu.make_async_copy(source, bufs.at[part], in_sem.at[b])

    def put(b):
        part = pl.ds(b * step, step)
        return pltpu.make_async_copy(bufs.at[part], out.at[part], out_sem.at[b])

    pieces = rows // step
    for b in range(pieces):
        fetch(b).start()
    block = lax.broadcasted_iota(jnp.int32, (1, width), 1) // BS
    masks = []
    for p in range(mask_ref.shape[0]):
        lanes = jnp.zeros((1, width), jnp.float32)
        for k in range(mask_ref.shape[2]):
            lanes = jnp.where(block == k, mask_ref[p, 0, k].astype(jnp.float32), lanes)
        masks.append(lanes.astype(jnp.bfloat16))
    for b in range(pieces):
        fetch(b).wait()
        mask = masks[(b * step) // BS]

        def scale(i, carry, mask=mask, b=b):
            row = b * step + i
            bufs[row] = bufs[row] * mask
            return carry

        lax.fori_loop(0, step, scale, 0, unroll=4)
        put(b).start()
    for b in range(pieces):
        put(b).wait()


def raw_slice(tc, center_mask):
    rows, _, width = tc.shape
    pieces = 8
    return pl.pallas_call(
        raw_kernel_send,
        in_specs=[pl.BlockSpec(memory_space=pltpu.SMEM), HBM],
        out_specs=HBM,
        out_shape=jax.ShapeDtypeStruct((rows, RAW_STEP, width), tc.dtype),
        scratch_shapes=[
            pltpu.VMEM((rows, RAW_STEP, width), tc.dtype),
            pltpu.SemaphoreType.DMA((pieces,)),
            pltpu.SemaphoreType.DMA((pieces,)),
        ],
        compiler_params=params(HALF_MIB),
        cost_estimate=cost(FIT_COST),
    )(center_mask, tc)


def fit_tile(pieces, metric_ref, scratch, pitch, count):
    metric = metric_ref[...]
    rows = metric.shape[0]

    def fit(pair, carry):
        columns = [jnp.concatenate(pieces(m), axis=0) for m in (2 * pair, 2 * pair + 1)]
        y = jnp.dot(metric, jnp.concatenate(columns, axis=1), preferred_element_type=jnp.float32)
        scratch[pl.ds(2 * pair, rows, stride=pitch), :] = y[:, :SIG]
        scratch[pl.ds(2 * pair + 1, rows, stride=pitch), :] = y[:, SIG:]
        return carry

    lax.fori_loop(0, count // 2, fit, 0, unroll=8)


def raw_kernel(metric_ref, dens_ref, raw, *refs):
    own, near, refs = refs[:2], refs[2:4], refs[4:]
    fitted, zero_ref, raw_buf, far_buf, own_buf, near_buf, staged, half_scratch, scratch = refs[:9]
    raw_sem, in_sem, out_sem = refs[9:]
    tiles, rows, count, _ = staged.shape
    pitch = count + 1
    blocks = rows // PB

    def fetch_raw(b):
        part = pl.ds(b * PB, PB)
        return pltpu.make_async_copy(raw.at[part], raw_buf.at[part], raw_sem.at[b])

    def fetch(t):
        k, at = t // 2, t % 2
        return [
            pltpu.make_async_copy(own[k].at[at], own_buf.at[t], in_sem.at[0, t]),
            pltpu.make_async_copy(near[k].at[at], near_buf.at[t], in_sem.at[1, t]),
        ]

    def put(t):
        lanes = pl.ds(t * SIG, SIG)
        return pltpu.make_async_copy(
            staged.at[t], fitted.at[:, pl.ds(RAW_MU, count), lanes], out_sem.at[t]
        )

    for b in range(blocks):
        fetch_raw(b).start()
    for t in range(tiles):
        for copy in fetch(t):
            copy.start()
    zero_ref[...] = jnp.zeros(zero_ref.shape, jnp.float32)

    def step(b, carry):
        fetch_raw(b).wait()
        half_rows(raw_buf[pl.ds(b * PB, PB)], dens_ref[...], half_scratch, count)
        for t in range(tiles):
            for m in range(count):
                far_buf[t, b, m] = turned(half_scratch, t, m, count)
        return carry

    lax.fori_loop(0, blocks, step, 0)
    for t in range(tiles):
        for copy in fetch(t):
            copy.wait()

        def pieces(m, t=t):
            return [buf[t, :, m].reshape(rows, SIG) for buf in (far_buf, own_buf, near_buf)]

        fit_tile(pieces, metric_ref, scratch, pitch, count)

        def store(block, inner, t=t):
            for q in range(QB):
                row = block * QB + q
                staged[t, row] = scratch[pl.ds(row * pitch, count), :].astype(jnp.bfloat16)
            return inner

        lax.fori_loop(0, rows // QB, store, 0)
        put(t).start()
    for t in range(tiles):
        put(t).wait()


def raw_call(raw_far, own, near, dens, metric, tc, cols):
    rows, count, width = raw_far.shape
    tiles = width // SIG
    buf = pltpu.VMEM((tiles, rows // PB, count, PB, SIG), jnp.bfloat16)
    return pl.pallas_call(
        raw_kernel,
        in_specs=[WHOLE, WHOLE] + [HBM] * 5,
        out_specs=[HBM, WHOLE],
        out_shape=[
            jax.ShapeDtypeStruct(tc.shape, jnp.bfloat16),
            jax.ShapeDtypeStruct((cols, cols), jnp.float32),
        ],
        scratch_shapes=[
            pltpu.VMEM(raw_far.shape, jnp.bfloat16),
            buf,
            buf,
            buf,
            pltpu.VMEM((tiles, rows, count, SIG), jnp.bfloat16),
            pltpu.VMEM((tiles, PB * (count + 1) + 8, SIG), jnp.float32),
            pltpu.VMEM((rows * (count + 1), SIG), jnp.float32),
            pltpu.SemaphoreType.DMA((rows // PB,)),
            pltpu.SemaphoreType.DMA((2, tiles)),
            pltpu.SemaphoreType.DMA((tiles,)),
        ],
        compiler_params=params(RAW_MIB),
        cost_estimate=cost(FIT_COST),
    )(metric, dens, raw_far, *own, *near)


def fit_kernel(chunk, raws, role, metric_ref, mask_ref, acc_ref, far, *refs):
    s, tiles, mu0, count = chunk
    (own, near, tc, _, fitted, exch_ref), refs = refs[:6], refs[6:]
    if role == "second":
        own_buf, near_buf, tc_buf = own, near, tc
        base = mu0
        far_buf, raw_buf, staged, scratch, out_sem, in_sem = refs
    else:
        own_buf, near_buf, tc_buf, far_buf, raw_buf, staged, scratch, out_sem, in_sem = refs
        base = 0
    rows = metric_ref.shape[0]
    pitch = count + 1
    wide = own_buf.shape[2]

    def fetch(t):
        part = pl.ds(mu0, wide)
        lanes = pl.ds(s + t * SIG, SIG)
        tile = s // SIG + t
        copies = [pltpu.make_async_copy(far.at[t], far_buf.at[t], in_sem.at[0, t])]
        if raws:
            source = fitted.at[:, pl.ds(RAW_MU, RAW_STEP), lanes]
            copies.append(pltpu.make_async_copy(source, raw_buf.at[t], in_sem.at[4, t]))
        if role == "second":
            return copies
        return copies + [
            pltpu.make_async_copy(own.at[tile, :, part], own_buf.at[t], in_sem.at[1, t]),
            pltpu.make_async_copy(near.at[tile, :, part], near_buf.at[t], in_sem.at[2, t]),
            pltpu.make_async_copy(tc.at[:, :, lanes], tc_buf.at[t], in_sem.at[3, t]),
        ]

    def put(t):
        lanes = pl.ds(s + t * SIG, SIG)
        return pltpu.make_async_copy(
            staged.at[t], fitted.at[:, pl.ds(mu0, count), lanes], out_sem.at[t]
        )

    for t in range(tiles):
        for copy in fetch(t):
            copy.start()
    exch_ref[...] = acc_ref[...]
    for t in range(tiles):
        for copy in fetch(t):
            copy.wait()

        def pieces(m, t=t):
            bufs = (far_buf[t, :, m], own_buf[t, :, base + m], near_buf[t, :, base + m])
            return [piece.reshape(rows, SIG) for piece in bufs]

        fit_tile(pieces, metric_ref, scratch, pitch, count)
        def contract(block, total, t=t):
            first = pl.multiple_of(block * QB, QB)
            lanes = slice(s + t * SIG, s + (t + 1) * SIG)
            mask = mask_ref[(block * QB) // BS, :, lanes].astype(jnp.bfloat16)
            left = []
            for q in range(QB):
                f = scratch[pl.ds((first + q) * pitch, count), :].astype(jnp.bfloat16)
                staged[t, first + q] = f
                if raws:
                    f = jnp.concatenate([f, raw_buf[t, first + q]], axis=0)
                left.append(f * mask)
            right = [tc_buf[t, first + q] for q in range(QB)]
            return total + lax.dot_general(
                jnp.concatenate(left, axis=1),
                jnp.concatenate(right, axis=1),
                (((1,), (1,)), ((), ())),
                preferred_element_type=jnp.float32,
            )

        lines = count + raws * RAW_STEP
        total = lax.fori_loop(
            0, rows // QB, contract, jnp.zeros((lines, acc_ref.shape[1]), jnp.float32), unroll=2
        )
        put(t).start()
        exch_ref[mu0:mu0 + count, :] += total[:count]
        if raws:
            exch_ref[RAW_MU:, :] += total[count:]
    for t in range(tiles):
        put(t).wait()


def fit_call(chunk, role, far, own, near, metric, tc, mask, acc, fitted):
    _, tiles, _, count = chunk
    rows, cols = metric.shape[0], acc.shape[1]
    raws = 0 if role == "second" else 1
    args = [metric, mask, acc, far, own, near, tc, fitted]
    operand = WHOLE if role == "second" else HBM
    wide = 2 * count if role == "first" else count
    fetched = [
        (tiles, rows // PB, wide, PB, SIG),
        (tiles, rows // PB, wide, PB, SIG),
        (tiles, rows, cols, SIG),
    ]
    handed = fetched if role == "first" else []
    kept = fetched if role == "" else []
    return pl.pallas_call(
        lambda *refs: fit_kernel(chunk, raws, role, *refs),
        in_specs=[WHOLE] * 3 + [HBM] + [operand] * 3 + [HBM],
        out_specs=[HBM, WHOLE] + [WHOLE] * len(handed),
        out_shape=[
            jax.ShapeDtypeStruct(fitted.shape, jnp.bfloat16),
            jax.ShapeDtypeStruct(acc.shape, jnp.float32),
        ] + [jax.ShapeDtypeStruct(shape, jnp.bfloat16) for shape in handed],
        scratch_shapes=[pltpu.VMEM(shape, jnp.bfloat16) for shape in kept] + [
            pltpu.VMEM(far.shape, jnp.bfloat16),
            pltpu.VMEM((tiles, rows, RAW_STEP if raws else 16, SIG), jnp.bfloat16),
            pltpu.VMEM((tiles, rows, count, SIG), jnp.bfloat16),
            pltpu.VMEM((rows * (count + 1), SIG), jnp.float32),
            pltpu.SemaphoreType.DMA((tiles,)),
            pltpu.SemaphoreType.DMA((5, tiles)),
        ],
        input_output_aliases={len(args) - 1: 0},
        compiler_params=params(FIT_MIB),
        cost_estimate=cost(FIT_COST),
    )(*args)


def sum_pa(value):
    size = lax.axis_size("pa")

    for stride, mask in ((1, 1), (2, 1), (2, 3), (8, 1), (8, 3)):
        pairs = [(i, i ^ (mask * stride)) for i in range(size)]
        value = value + lax.ppermute(value, "pa", pairs)
    return value


def after(value, *earlier):
    return lax.optimization_barrier((value,) + earlier)[0]


def on_device(three_center, center_mask, density, density_mask, metric_band):
    rows, cols, width = three_center.shape
    size = lax.axis_size("pa")
    near_pairs = [(i, i ^ 1) for i in range(size)]
    far_pairs = [(i, i + 1 if i % 2 else i - 1) for i in range(1, size - 1)]

    def to_far(value, *earlier):
        return lax.ppermute(after(value, *earlier), "pa", far_pairs)

    raw = raw_slice(three_center, center_mask)
    raw_far = to_far(raw)
    mask = jnp.repeat(center_mask, BS, axis=2).astype(jnp.float32)
    block_mask = jnp.repeat(jnp.repeat(density_mask, BS, axis=0), BS, axis=1)
    local = after(density * block_mask.astype(jnp.bfloat16), raw)
    count = lax.axis_size("mu")
    parts = [local] + [
        lax.ppermute(local, "mu", [((i + k) % count, i) for i in range(count)])
        for k in range(1, count)
    ]
    left, middle, right = jnp.split(metric_band, 3, axis=1)
    metric = jnp.where(
        lax.axis_index("pa") % 2 == 0,
        metric_band,
        jnp.concatenate([right, middle, left], axis=1),
    )

    def to_near(value):
        return lax.ppermute(value, "pa", near_pairs)

    dens, low, *rest = half_call(three_center, mask, parts)
    own_raw, chunks = rest[:2], rest[2:]
    far = [to_far(chunks[0])]
    near_raw = [to_near(piece) for piece in own_raw]
    near_low = to_near(low)
    fitted, acc = raw_call(raw_far, own_raw, near_raw, dens, metric, three_center, cols)
    far += [to_far(chunks[1], acc), to_far(chunks[2], acc)]
    handed = (low, near_low, three_center)
    for c, chunk in enumerate(CHUNKS):
        role = {len(CHUNKS) - 2: "first", len(CHUNKS) - 1: "second"}.get(c, "")
        fitted, acc, *rest = fit_call(
            chunk, role, far[c], *handed[:2], metric, handed[2], mask, acc, fitted
        )
        handed = tuple(rest) or handed
        if len(far) < len(CHUNKS):
            far.append(to_far(chunks[len(far)], acc))
    scale = 1.0 / math.sqrt(rows * size * width)
    return (fitted, sum_pa(acc) * scale)


def solution(mesh):
    placed = (P("pa", "mu", None), P("pa", "mu", None), P("mu", None), P("mu", None), P("pa", None))
    return jax.shard_map(
        on_device,
        mesh=mesh,
        in_specs=placed,
        out_specs=(P("pa", "mu", None), P("mu", None)),
        check_vma=False,
    )
```

```python
import math

import jax
import jax.numpy as jnp
from jax import lax
from jax.experimental import pallas as pl
from jax.experimental.pallas import tpu as pltpu
from jax.sharding import PartitionSpec as P

BS = 64
SIG = 128
PB = 16
QB = 16
MIB = 2**20

RAW_MU = 32
RAW_STEP = 32
LOW = (0, 4, 0, 32)
RAW_HALVES = ((0, 2, 32, 32), (256, 2, 32, 32))
CHUNKS = ((0, 2, 0, 32), (256, 1, 0, 32), (384, 1, 0, 16), (384, 1, 16, 16))
PIECES = (LOW,) + RAW_HALVES + CHUNKS
HALF_MIB = 56
HALF_COST = 1
FIT_MIB = 40
RAW_MIB = 32
FIT_COST = 0.3
HBM = pl.BlockSpec(memory_space=pltpu.HBM)
WHOLE = pl.BlockSpec(memory_space=pltpu.VMEM)


def cost(us):
    return pl.CostEstimate(
        flops=int(us * 4e9), bytes_accessed=int(us * 12e6), transcendentals=0
    )


def params(mib):
    return pltpu.CompilerParams(vmem_limit_bytes=mib * MIB)


def half_rows(x, dens, scratch, cols):
    flat = jnp.dot(x.reshape(PB * cols, x.shape[2]), dens, preferred_element_type=jnp.float32)
    pitch = cols + 1
    for t in range(scratch.shape[0]):
        for p in range(PB):
            scratch[t, p * pitch:p * pitch + cols] = flat[
                p * cols:(p + 1) * cols, t * SIG:(t + 1) * SIG
            ]


def turned(scratch, t, m, cols):
    return scratch[t, pl.ds(m, PB, stride=cols + 1), :].astype(jnp.bfloat16)


def half_kernel(mask_ref, *refs):
    parts, tc_hbm = refs[:4], refs[4]
    dens_ref, outs = refs[5], refs[6:-5]
    tc_buf, staged, scratch, in_sem, out_sem = refs[-5:]
    rows, cols, width = tc_buf.shape
    blocks = rows // PB

    def fetch(b):
        rows_b = pl.ds(b * PB, PB)
        return pltpu.make_async_copy(tc_hbm.at[rows_b], tc_buf.at[rows_b], in_sem.at[b])

    for b in range(blocks):
        fetch(b).start()
    me = lax.axis_index("mu")
    depth = parts[0].shape[0]
    for k, part in enumerate(parts):
        at = lax.rem(me + k, len(parts)) * depth
        dens_ref[pl.ds(pl.multiple_of(at, depth), depth), :] = part[...]

    def step(b, carry):
        fetch(b).wait()
        x = tc_buf[pl.ds(b * PB, PB)] * mask_ref[(b * PB) // BS].astype(jnp.bfloat16)
        half_rows(x, dens_ref[...], scratch, cols)
        for t in range(width // SIG):
            for m in range(cols):
                staged[t, b, m] = turned(scratch, t, m, cols)
        for k, (s, tiles, mu0, count) in enumerate(PIECES):
            part = staged.at[pl.ds(s // SIG, tiles), b, pl.ds(mu0, count)]
            pltpu.make_async_copy(part, outs[k].at[:, b], out_sem.at[k]).start()
        return carry

    lax.fori_loop(0, blocks, step, 0)
    for k, (s, tiles, mu0, count) in enumerate(PIECES):
        part = staged.at[pl.ds(s // SIG, tiles), :, pl.ds(mu0, count)]
        pltpu.make_async_copy(part, outs[k], out_sem.at[k]).wait()


def half_call(tc, mask, parts):
    rows, cols, width = tc.shape
    whole = (width // SIG, rows // PB, cols, PB, SIG)
    shapes = [(width, width)] + [(t, rows // PB, n, PB, SIG) for _, t, _, n in PIECES]
    return pl.pallas_call(
        half_kernel,
        in_specs=[WHOLE] * (1 + len(parts)) + [HBM],
        out_specs=[WHOLE] + [HBM] * len(PIECES),
        out_shape=[jax.ShapeDtypeStruct(shape, jnp.bfloat16) for shape in shapes],
        scratch_shapes=[
            pltpu.VMEM(tc.shape, jnp.bfloat16),
            pltpu.VMEM(whole, jnp.bfloat16),
            pltpu.VMEM((width // SIG, (PB + 1) * (cols + 1) + 8, SIG), jnp.float32),
            pltpu.SemaphoreType.DMA((rows // PB,)),
            pltpu.SemaphoreType.DMA((len(PIECES),)),
        ],
        compiler_params=params(HALF_MIB),
        cost_estimate=cost(HALF_COST),
    )(mask, *parts, tc)


def raw_kernel_send(mask_ref, tc, out, bufs, in_sem, out_sem):
    rows, count, width = bufs.shape
    step = rows // in_sem.shape[0]

    def fetch(b):
        part = pl.ds(b * step, step)
        source = tc.at[part, pl.ds(RAW_MU, RAW_STEP)]
        return pltpu.make_async_copy(source, bufs.at[part], in_sem.at[b])

    def put(b):
        part = pl.ds(b * step, step)
        return pltpu.make_async_copy(bufs.at[part], out.at[part], out_sem.at[b])

    pieces = rows // step
    for b in range(pieces):
        fetch(b).start()
    block = lax.broadcasted_iota(jnp.int32, (1, width), 1) // BS
    masks = []
    for p in range(mask_ref.shape[0]):
        lanes = jnp.zeros((1, width), jnp.float32)
        for k in range(mask_ref.shape[2]):
            lanes = jnp.where(block == k, mask_ref[p, 0, k].astype(jnp.float32), lanes)
        masks.append(lanes.astype(jnp.bfloat16))
    for b in range(pieces):
        fetch(b).wait()
        mask = masks[(b * step) // BS]

        def scale(i, carry, mask=mask, b=b):
            row = b * step + i
            bufs[row] = bufs[row] * mask
            return carry

        lax.fori_loop(0, step, scale, 0, unroll=4)
        put(b).start()
    for b in range(pieces):
        put(b).wait()


def raw_slice(tc, center_mask):
    rows, _, width = tc.shape
    pieces = 4
    return pl.pallas_call(
        raw_kernel_send,
        in_specs=[pl.BlockSpec(memory_space=pltpu.SMEM), HBM],
        out_specs=HBM,
        out_shape=jax.ShapeDtypeStruct((rows, RAW_STEP, width), tc.dtype),
        scratch_shapes=[
            pltpu.VMEM((rows, RAW_STEP, width), tc.dtype),
            pltpu.SemaphoreType.DMA((pieces,)),
            pltpu.SemaphoreType.DMA((pieces,)),
        ],
        compiler_params=params(HALF_MIB),
        cost_estimate=cost(FIT_COST),
    )(center_mask, tc)


def fit_tile(pieces, metric_ref, scratch, pitch, count):
    metric = metric_ref[...]
    rows = metric.shape[0]

    def fit(pair, carry):
        columns = [jnp.concatenate(pieces(m), axis=0) for m in (2 * pair, 2 * pair + 1)]
        y = jnp.dot(metric, jnp.concatenate(columns, axis=1), preferred_element_type=jnp.float32)
        scratch[pl.ds(2 * pair, rows, stride=pitch), :] = y[:, :SIG]
        scratch[pl.ds(2 * pair + 1, rows, stride=pitch), :] = y[:, SIG:]
        return carry

    lax.fori_loop(0, count // 2, fit, 0, unroll=8)


def raw_kernel(metric_ref, dens_ref, raw, *refs):
    own, near, refs = refs[:2], refs[2:4], refs[4:]
    fitted, zero_ref, raw_buf, far_buf, own_buf, near_buf, staged, half_scratch, scratch = refs[:9]
    raw_sem, in_sem, out_sem = refs[9:]
    tiles, rows, count, _ = staged.shape
    pitch = count + 1
    blocks = rows // PB

    def fetch_raw(b):
        part = pl.ds(b * PB, PB)
        return pltpu.make_async_copy(raw.at[part], raw_buf.at[part], raw_sem.at[b])

    def fetch(t):
        k, at = t // 2, t % 2
        return [
            pltpu.make_async_copy(own[k].at[at], own_buf.at[t], in_sem.at[0, t]),
            pltpu.make_async_copy(near[k].at[at], near_buf.at[t], in_sem.at[1, t]),
        ]

    def put(t):
        lanes = pl.ds(t * SIG, SIG)
        return pltpu.make_async_copy(
            staged.at[t], fitted.at[:, pl.ds(RAW_MU, count), lanes], out_sem.at[t]
        )

    for b in range(blocks):
        fetch_raw(b).start()
    for t in range(tiles):
        for copy in fetch(t):
            copy.start()
    zero_ref[...] = jnp.zeros(zero_ref.shape, jnp.float32)

    def step(b, carry):
        fetch_raw(b).wait()
        half_rows(raw_buf[pl.ds(b * PB, PB)], dens_ref[...], half_scratch, count)
        for t in range(tiles):
            for m in range(count):
                far_buf[t, b, m] = turned(half_scratch, t, m, count)
        return carry

    lax.fori_loop(0, blocks, step, 0)
    for t in range(tiles):
        for copy in fetch(t):
            copy.wait()

        def pieces(m, t=t):
            return [buf[t, :, m].reshape(rows, SIG) for buf in (far_buf, own_buf, near_buf)]

        fit_tile(pieces, metric_ref, scratch, pitch, count)

        def store(block, inner, t=t):
            for q in range(QB):
                row = block * QB + q
                staged[t, row] = scratch[pl.ds(row * pitch, count), :].astype(jnp.bfloat16)
            return inner

        lax.fori_loop(0, rows // QB, store, 0)
        put(t).start()
    for t in range(tiles):
        put(t).wait()


def raw_call(raw_far, own, near, dens, metric, tc, cols):
    rows, count, width = raw_far.shape
    tiles = width // SIG
    buf = pltpu.VMEM((tiles, rows // PB, count, PB, SIG), jnp.bfloat16)
    return pl.pallas_call(
        raw_kernel,
        in_specs=[WHOLE, WHOLE] + [HBM] * 5,
        out_specs=[HBM, WHOLE],
        out_shape=[
            jax.ShapeDtypeStruct(tc.shape, jnp.bfloat16),
            jax.ShapeDtypeStruct((cols, cols), jnp.float32),
        ],
        scratch_shapes=[
            pltpu.VMEM(raw_far.shape, jnp.bfloat16),
            buf,
            buf,
            buf,
            pltpu.VMEM((tiles, rows, count, SIG), jnp.bfloat16),
            pltpu.VMEM((tiles, (PB + 1) * (count + 1) + 8, SIG), jnp.float32),
            pltpu.VMEM(((rows + 1) * (count + 1) + 8, SIG), jnp.float32),
            pltpu.SemaphoreType.DMA((rows // PB,)),
            pltpu.SemaphoreType.DMA((2, tiles)),
            pltpu.SemaphoreType.DMA((tiles,)),
        ],
        compiler_params=params(RAW_MIB),
        cost_estimate=cost(FIT_COST),
    )(metric, dens, raw_far, *own, *near)


def fit_kernel(chunk, raws, role, metric_ref, mask_ref, acc_ref, far, *refs):
    s, tiles, mu0, count = chunk
    (own, near, tc, _, fitted, exch_ref), refs = refs[:6], refs[6:]
    if role == "second":
        own_buf, near_buf, tc_buf = own, near, tc
        base = mu0
        far_buf, raw_buf, staged, scratch, out_sem, in_sem = refs
    else:
        own_buf, near_buf, tc_buf, far_buf, raw_buf, staged, scratch, out_sem, in_sem = refs
        base = 0
    rows = metric_ref.shape[0]
    pitch = count + 1
    wide = own_buf.shape[2]

    def fetch(t):
        part = pl.ds(mu0, wide)
        lanes = pl.ds(s + t * SIG, SIG)
        tile = s // SIG + t
        copies = [pltpu.make_async_copy(far.at[t], far_buf.at[t], in_sem.at[0, t])]
        if raws:
            source = fitted.at[:, pl.ds(RAW_MU, RAW_STEP), lanes]
            copies.append(pltpu.make_async_copy(source, raw_buf.at[t], in_sem.at[4, t]))
        if role == "second":
            return copies
        return copies + [
            pltpu.make_async_copy(own.at[tile, :, part], own_buf.at[t], in_sem.at[1, t]),
            pltpu.make_async_copy(near.at[tile, :, part], near_buf.at[t], in_sem.at[2, t]),
            pltpu.make_async_copy(tc.at[:, :, lanes], tc_buf.at[t], in_sem.at[3, t]),
        ]

    def put(t):
        lanes = pl.ds(s + t * SIG, SIG)
        return pltpu.make_async_copy(
            staged.at[t], fitted.at[:, pl.ds(mu0, count), lanes], out_sem.at[t]
        )

    for t in range(tiles):
        for copy in fetch(t):
            copy.start()
    exch_ref[...] = acc_ref[...]
    for t in range(tiles):
        for copy in fetch(t):
            copy.wait()

        def pieces(m, t=t):
            bufs = (far_buf[t, :, m], own_buf[t, :, base + m], near_buf[t, :, base + m])
            return [piece.reshape(rows, SIG) for piece in bufs]

        fit_tile(pieces, metric_ref, scratch, pitch, count)
        def contract(block, total, t=t):
            first = pl.multiple_of(block * QB, QB)
            lanes = slice(s + t * SIG, s + (t + 1) * SIG)
            mask = mask_ref[(block * QB) // BS, :, lanes].astype(jnp.bfloat16)
            left = []
            for q in range(QB):
                f = scratch[pl.ds((first + q) * pitch, count), :].astype(jnp.bfloat16)
                staged[t, first + q] = f
                if raws:
                    f = jnp.concatenate([f, raw_buf[t, first + q]], axis=0)
                left.append(f * mask)
            right = [tc_buf[t, first + q] for q in range(QB)]
            return total + lax.dot_general(
                jnp.concatenate(left, axis=1),
                jnp.concatenate(right, axis=1),
                (((1,), (1,)), ((), ())),
                preferred_element_type=jnp.float32,
            )

        lines = count + raws * RAW_STEP
        total = lax.fori_loop(
            0, rows // QB, contract, jnp.zeros((lines, acc_ref.shape[1]), jnp.float32), unroll=2
        )
        put(t).start()
        exch_ref[mu0:mu0 + count, :] += total[:count]
        if raws:
            exch_ref[RAW_MU:, :] += total[count:]
    for t in range(tiles):
        put(t).wait()


def fit_call(chunk, role, far, own, near, metric, tc, mask, acc, fitted):
    _, tiles, _, count = chunk
    rows, cols = metric.shape[0], acc.shape[1]
    raws = 0 if role == "second" else 1
    args = [metric, mask, acc, far, own, near, tc, fitted]
    operand = WHOLE if role == "second" else HBM
    wide = 2 * count if role == "first" else count
    fetched = [
        (tiles, rows // PB, wide, PB, SIG),
        (tiles, rows // PB, wide, PB, SIG),
        (tiles, rows, cols, SIG),
    ]
    handed = fetched if role == "first" else []
    kept = fetched if role == "" else []
    return pl.pallas_call(
        lambda *refs: fit_kernel(chunk, raws, role, *refs),
        in_specs=[WHOLE] * 3 + [HBM] + [operand] * 3 + [HBM],
        out_specs=[HBM, WHOLE] + [WHOLE] * len(handed),
        out_shape=[
            jax.ShapeDtypeStruct(fitted.shape, jnp.bfloat16),
            jax.ShapeDtypeStruct(acc.shape, jnp.float32),
        ] + [jax.ShapeDtypeStruct(shape, jnp.bfloat16) for shape in handed],
        scratch_shapes=[pltpu.VMEM(shape, jnp.bfloat16) for shape in kept] + [
            pltpu.VMEM(far.shape, jnp.bfloat16),
            pltpu.VMEM((tiles, rows, RAW_STEP if raws else 16, SIG), jnp.bfloat16),
            pltpu.VMEM((tiles, rows, count, SIG), jnp.bfloat16),
            pltpu.VMEM(((rows + 1) * (count + 1) + 8, SIG), jnp.float32),
            pltpu.SemaphoreType.DMA((tiles,)),
            pltpu.SemaphoreType.DMA((5, tiles)),
        ],
        input_output_aliases={len(args) - 1: 0},
        compiler_params=params(FIT_MIB),
        cost_estimate=cost(FIT_COST),
    )(*args)


def sum_pa(value):
    size = lax.axis_size("pa")

    for stride, mask in ((1, 1), (2, 1), (2, 3), (8, 1), (8, 3)):
        pairs = [(i, i ^ (mask * stride)) for i in range(size)]
        value = value + lax.ppermute(value, "pa", pairs)
    return value


def after(value, *earlier):
    return lax.optimization_barrier((value,) + earlier)[0]


def on_device(three_center, center_mask, density, density_mask, metric_band):
    rows, cols, width = three_center.shape
    size = lax.axis_size("pa")
    near_pairs = [(i, i ^ 1) for i in range(size)]
    far_pairs = [(i, i + 1 if i % 2 else i - 1) for i in range(1, size - 1)]

    def to_far(value, *earlier):
        return lax.ppermute(after(value, *earlier), "pa", far_pairs)

    raw = raw_slice(three_center, center_mask)
    raw_far = to_far(raw)
    mask = jnp.repeat(center_mask, BS, axis=2).astype(jnp.float32)
    block_mask = jnp.repeat(jnp.repeat(density_mask, BS, axis=0), BS, axis=1)
    local = after(density * block_mask.astype(jnp.bfloat16), raw)
    count = lax.axis_size("mu")
    parts = [local] + [
        lax.ppermute(local, "mu", [((i + k) % count, i) for i in range(count)])
        for k in range(1, count)
    ]
    left, middle, right = jnp.split(metric_band, 3, axis=1)
    metric = jnp.where(
        lax.axis_index("pa") % 2 == 0,
        metric_band,
        jnp.concatenate([right, middle, left], axis=1),
    )

    def to_near(value):
        return lax.ppermute(value, "pa", near_pairs)

    dens, low, *rest = half_call(three_center, mask, parts)
    own_raw, chunks = rest[:2], rest[2:]
    far = [to_far(chunks[0])]
    near_raw = [to_near(piece) for piece in own_raw]
    near_low = to_near(low)
    fitted, acc = raw_call(raw_far, own_raw, near_raw, dens, metric, three_center, cols)
    far += [to_far(chunks[1], acc), to_far(chunks[2], acc)]
    handed = (low, near_low, three_center)
    for c, chunk in enumerate(CHUNKS):
        role = {len(CHUNKS) - 2: "first", len(CHUNKS) - 1: "second"}.get(c, "")
        fitted, acc, *rest = fit_call(
            chunk, role, far[c], *handed[:2], metric, handed[2], mask, acc, fitted
        )
        handed = tuple(rest) or handed
        if len(far) < len(CHUNKS):
            far.append(to_far(chunks[len(far)], acc))
    scale = 1.0 / math.sqrt(rows * size * width)
    return (fitted, sum_pa(acc) * scale)


def solution(mesh):
    placed = (P("pa", "mu", None), P("pa", "mu", None), P("mu", None), P("mu", None), P("pa", None))
    return jax.shard_map(
        on_device,
        mesh=mesh,
        in_specs=placed,
        out_specs=(P("pa", "mu", None), P("mu", None)),
        check_vma=False,
    )
```

```python
import math

import jax
import jax.numpy as jnp
from jax import lax
from jax.experimental import pallas as pl
from jax.experimental.pallas import tpu as pltpu
from jax.sharding import PartitionSpec as P

BS = 64
SIG = 128
PB = 16
QB = 16
MIB = 2**20

RAW_MU = 32
RAW_STEP = 32
LOW = (0, 4, 0, 32)
RAW_HALVES = ((0, 2, 32, 32), (256, 2, 32, 32))
CHUNKS = ((0, 2, 0, 32), (256, 1, 0, 32), (384, 1, 0, 16), (384, 1, 16, 16))
PIECES = (LOW,) + RAW_HALVES + CHUNKS
HALF_MIB = 56
HALF_COST = 1
FIT_MIB = 40
RAW_MIB = 32
FIT_COST = 0.3
HBM = pl.BlockSpec(memory_space=pltpu.HBM)
WHOLE = pl.BlockSpec(memory_space=pltpu.VMEM)


def cost(us):
    return pl.CostEstimate(
        flops=int(us * 4e9), bytes_accessed=int(us * 12e6), transcendentals=0
    )


def params(mib):
    return pltpu.CompilerParams(vmem_limit_bytes=mib * MIB)


def half_rows(x, dens, scratch, cols):
    flat = jnp.dot(x.reshape(PB * cols, x.shape[2]), dens, preferred_element_type=jnp.float32)
    pitch = cols + 1
    for t in range(scratch.shape[0]):
        for p in range(PB):
            scratch[t, p * pitch:p * pitch + cols] = flat[
                p * cols:(p + 1) * cols, t * SIG:(t + 1) * SIG
            ]


def turned(scratch, t, m, cols):
    return scratch[t, pl.ds(m, PB, stride=cols + 1), :].astype(jnp.bfloat16)


def half_kernel(mask_ref, *refs):
    parts, tc_hbm = refs[:4], refs[4]
    dens_ref, outs = refs[5], refs[6:-5]
    tc_buf, staged, scratch, in_sem, out_sem = refs[-5:]
    rows, cols, width = tc_buf.shape
    blocks = rows // PB

    def fetch(b):
        rows_b = pl.ds(b * PB, PB)
        return pltpu.make_async_copy(tc_hbm.at[rows_b], tc_buf.at[rows_b], in_sem.at[b])

    for b in range(blocks):
        fetch(b).start()
    me = lax.axis_index("mu")
    depth = parts[0].shape[0]
    for k, part in enumerate(parts):
        at = lax.rem(me + k, len(parts)) * depth
        dens_ref[pl.ds(pl.multiple_of(at, depth), depth), :] = part[...]

    def step(b, carry):
        fetch(b).wait()
        x = tc_buf[pl.ds(b * PB, PB)] * mask_ref[(b * PB) // BS].astype(jnp.bfloat16)
        half_rows(x, dens_ref[...], scratch, cols)
        for t in range(width // SIG):
            for m in range(cols):
                staged[t, b, m] = turned(scratch, t, m, cols)
        for k, (s, tiles, mu0, count) in enumerate(PIECES):
            part = staged.at[pl.ds(s // SIG, tiles), b, pl.ds(mu0, count)]
            pltpu.make_async_copy(part, outs[k].at[:, b], out_sem.at[k]).start()
        return carry

    lax.fori_loop(0, blocks, step, 0)
    for k, (s, tiles, mu0, count) in enumerate(PIECES):
        part = staged.at[pl.ds(s // SIG, tiles), :, pl.ds(mu0, count)]
        pltpu.make_async_copy(part, outs[k], out_sem.at[k]).wait()


def half_call(tc, mask, parts):
    rows, cols, width = tc.shape
    whole = (width // SIG, rows // PB, cols, PB, SIG)
    shapes = [(width, width)] + [(t, rows // PB, n, PB, SIG) for _, t, _, n in PIECES]
    return pl.pallas_call(
        half_kernel,
        in_specs=[WHOLE] * (1 + len(parts)) + [HBM],
        out_specs=[WHOLE] + [HBM] * len(PIECES),
        out_shape=[jax.ShapeDtypeStruct(shape, jnp.bfloat16) for shape in shapes],
        scratch_shapes=[
            pltpu.VMEM(tc.shape, jnp.bfloat16),
            pltpu.VMEM(whole, jnp.bfloat16),
            pltpu.VMEM((width // SIG, (PB + 1) * (cols + 1) + 8, SIG), jnp.float32),
            pltpu.SemaphoreType.DMA((rows // PB,)),
            pltpu.SemaphoreType.DMA((len(PIECES),)),
        ],
        compiler_params=params(HALF_MIB),
        cost_estimate=cost(HALF_COST),
    )(mask, *parts, tc)


def raw_kernel_send(mask_ref, tc, out, bufs, in_sem, out_sem):
    rows, count, width = bufs.shape
    step = rows // in_sem.shape[0]

    def fetch(b):
        part = pl.ds(b * step, step)
        source = tc.at[part, pl.ds(RAW_MU, RAW_STEP)]
        return pltpu.make_async_copy(source, bufs.at[part], in_sem.at[b])

    def put(b):
        part = pl.ds(b * step, step)
        return pltpu.make_async_copy(bufs.at[part], out.at[part], out_sem.at[b])

    pieces = rows // step
    for b in range(pieces):
        fetch(b).start()
    block = lax.broadcasted_iota(jnp.int32, (1, width), 1) // BS
    masks = []
    for p in range(mask_ref.shape[0]):
        lanes = jnp.zeros((1, width), jnp.float32)
        for k in range(mask_ref.shape[2]):
            lanes = jnp.where(block == k, mask_ref[p, 0, k].astype(jnp.float32), lanes)
        masks.append(lanes.astype(jnp.bfloat16))
    for b in range(pieces):
        fetch(b).wait()
        mask = masks[(b * step) // BS]

        def scale(i, carry, mask=mask, b=b):
            row = b * step + i
            bufs[row] = bufs[row] * mask
            return carry

        lax.fori_loop(0, step, scale, 0, unroll=4)
        put(b).start()
    for b in range(pieces):
        put(b).wait()


def raw_slice(tc, center_mask):
    rows, _, width = tc.shape
    pieces = 4
    return pl.pallas_call(
        raw_kernel_send,
        in_specs=[pl.BlockSpec(memory_space=pltpu.SMEM), HBM],
        out_specs=HBM,
        out_shape=jax.ShapeDtypeStruct((rows, RAW_STEP, width), tc.dtype),
        scratch_shapes=[
            pltpu.VMEM((rows, RAW_STEP, width), tc.dtype),
            pltpu.SemaphoreType.DMA((pieces,)),
            pltpu.SemaphoreType.DMA((pieces,)),
        ],
        compiler_params=params(HALF_MIB),
        cost_estimate=cost(FIT_COST),
    )(center_mask, tc)


def fit_tile(pieces, metric_ref, scratch, pitch, count):
    metric = metric_ref[...]
    rows = metric.shape[0]

    def fit(pair, carry):
        columns = [jnp.concatenate(pieces(m), axis=0) for m in (2 * pair, 2 * pair + 1)]
        y = jnp.dot(metric, jnp.concatenate(columns, axis=1), preferred_element_type=jnp.float32)
        scratch[pl.ds(2 * pair, rows, stride=pitch), :] = y[:, :SIG]
        scratch[pl.ds(2 * pair + 1, rows, stride=pitch), :] = y[:, SIG:]
        return carry

    lax.fori_loop(0, count // 2, fit, 0, unroll=8)


def raw_kernel(metric_ref, dens_ref, raw, *refs):
    own, near, refs = refs[:2], refs[2:4], refs[4:]
    fitted, zero_ref, raw_buf, far_buf, own_buf, near_buf, staged, half_scratch, scratch = refs[:9]
    raw_sem, in_sem, out_sem = refs[9:]
    tiles, rows, count, _ = staged.shape
    pitch = count + 1
    blocks = rows // PB

    def fetch_raw(b):
        part = pl.ds(b * PB, PB)
        return pltpu.make_async_copy(raw.at[part], raw_buf.at[part], raw_sem.at[b])

    def fetch(t):
        k, at = t // 2, t % 2
        return [
            pltpu.make_async_copy(own[k].at[at], own_buf.at[t], in_sem.at[0, t]),
            pltpu.make_async_copy(near[k].at[at], near_buf.at[t], in_sem.at[1, t]),
        ]

    def put(t):
        lanes = pl.ds(t * SIG, SIG)
        return pltpu.make_async_copy(
            staged.at[t], fitted.at[:, pl.ds(RAW_MU, count), lanes], out_sem.at[t]
        )

    for b in range(blocks):
        fetch_raw(b).start()
    for t in range(tiles):
        for copy in fetch(t):
            copy.start()
    zero_ref[...] = jnp.zeros(zero_ref.shape, jnp.float32)

    def step(b, carry):
        fetch_raw(b).wait()
        half_rows(raw_buf[pl.ds(b * PB, PB)], dens_ref[...], half_scratch, count)
        for t in range(tiles):
            for m in range(count):
                far_buf[t, b, m] = turned(half_scratch, t, m, count)
        return carry

    lax.fori_loop(0, blocks, step, 0)
    for t in range(tiles):
        for copy in fetch(t):
            copy.wait()

        def pieces(m, t=t):
            return [buf[t, :, m].reshape(rows, SIG) for buf in (far_buf, own_buf, near_buf)]

        fit_tile(pieces, metric_ref, scratch, pitch, count)

        def store(block, inner, t=t):
            for q in range(QB):
                row = block * QB + q
                staged[t, row] = scratch[pl.ds(row * pitch, count), :].astype(jnp.bfloat16)
            return inner

        lax.fori_loop(0, rows // QB, store, 0)
        put(t).start()
    for t in range(tiles):
        put(t).wait()


def raw_call(raw_far, own, near, dens, metric, tc, cols):
    rows, count, width = raw_far.shape
    tiles = width // SIG
    buf = pltpu.VMEM((tiles, rows // PB, count, PB, SIG), jnp.bfloat16)
    return pl.pallas_call(
        raw_kernel,
        in_specs=[WHOLE, WHOLE] + [HBM] * 5,
        out_specs=[HBM, WHOLE],
        out_shape=[
            jax.ShapeDtypeStruct(tc.shape, jnp.bfloat16),
            jax.ShapeDtypeStruct((cols, cols), jnp.float32),
        ],
        scratch_shapes=[
            pltpu.VMEM(raw_far.shape, jnp.bfloat16),
            buf,
            buf,
            buf,
            pltpu.VMEM((tiles, rows, count, SIG), jnp.bfloat16),
            pltpu.VMEM((tiles, (PB + 1) * (count + 1) + 8, SIG), jnp.float32),
            pltpu.VMEM(((rows + 1) * (count + 1) + 8, SIG), jnp.float32),
            pltpu.SemaphoreType.DMA((rows // PB,)),
            pltpu.SemaphoreType.DMA((2, tiles)),
            pltpu.SemaphoreType.DMA((tiles,)),
        ],
        compiler_params=params(RAW_MIB),
        cost_estimate=cost(FIT_COST),
    )(metric, dens, raw_far, *own, *near)


def fit_kernel(chunk, raws, role, metric_ref, mask_ref, acc_ref, far, *refs):
    s, tiles, mu0, count = chunk
    (own, near, tc, _, fitted, exch_ref), refs = refs[:6], refs[6:]
    if role == "second":
        own_buf, near_buf, tc_buf = own, near, tc
        base = mu0
        far_buf, raw_buf, staged, scratch, out_sem, in_sem = refs
    else:
        own_buf, near_buf, tc_buf, far_buf, raw_buf, staged, scratch, out_sem, in_sem = refs
        base = 0
    rows = metric_ref.shape[0]
    pitch = count + 1
    wide = own_buf.shape[2]

    def fetch(t):
        part = pl.ds(mu0, wide)
        lanes = pl.ds(s + t * SIG, SIG)
        tile = s // SIG + t
        copies = [pltpu.make_async_copy(far.at[t], far_buf.at[t], in_sem.at[0, t])]
        if raws:
            source = fitted.at[:, pl.ds(RAW_MU, RAW_STEP), lanes]
            copies.append(pltpu.make_async_copy(source, raw_buf.at[t], in_sem.at[4, t]))
        if role == "second":
            return copies
        return copies + [
            pltpu.make_async_copy(own.at[tile, :, part], own_buf.at[t], in_sem.at[1, t]),
            pltpu.make_async_copy(near.at[tile, :, part], near_buf.at[t], in_sem.at[2, t]),
            pltpu.make_async_copy(tc.at[:, :, lanes], tc_buf.at[t], in_sem.at[3, t]),
        ]

    def put(t):
        lanes = pl.ds(s + t * SIG, SIG)
        return pltpu.make_async_copy(
            staged.at[t], fitted.at[:, pl.ds(mu0, count), lanes], out_sem.at[t]
        )

    for t in range(tiles):
        for copy in fetch(t):
            copy.start()
    exch_ref[...] = acc_ref[...]
    for t in range(tiles):
        for copy in fetch(t):
            copy.wait()

        def pieces(m, t=t):
            bufs = (far_buf[t, :, m], own_buf[t, :, base + m], near_buf[t, :, base + m])
            return [piece.reshape(rows, SIG) for piece in bufs]

        fit_tile(pieces, metric_ref, scratch, pitch, count)
        def contract(block, total, t=t):
            first = pl.multiple_of(block * QB, QB)
            lanes = slice(s + t * SIG, s + (t + 1) * SIG)
            mask = mask_ref[(block * QB) // BS, :, lanes].astype(jnp.bfloat16)
            left = []
            for q in range(QB):
                f = scratch[pl.ds((first + q) * pitch, count), :].astype(jnp.bfloat16)
                staged[t, first + q] = f
                if raws:
                    f = jnp.concatenate([f, raw_buf[t, first + q]], axis=0)
                left.append(f * mask)
            right = [tc_buf[t, first + q] for q in range(QB)]
            return total + lax.dot_general(
                jnp.concatenate(left, axis=1),
                jnp.concatenate(right, axis=1),
                (((1,), (1,)), ((), ())),
                preferred_element_type=jnp.float32,
            )

        lines = count + raws * RAW_STEP
        total = lax.fori_loop(
            0, rows // QB, contract, jnp.zeros((lines, acc_ref.shape[1]), jnp.float32), unroll=2
        )
        put(t).start()
        exch_ref[mu0:mu0 + count, :] += total[:count]
        if raws:
            exch_ref[RAW_MU:, :] += total[count:]
    for t in range(tiles):
        put(t).wait()


def fit_call(chunk, role, far, own, near, metric, tc, mask, acc, fitted):
    _, tiles, _, count = chunk
    rows, cols = metric.shape[0], acc.shape[1]
    raws = 0 if role == "second" else 1
    args = [metric, mask, acc, far, own, near, tc, fitted]
    operand = WHOLE if role == "second" else HBM
    wide = 2 * count if role == "first" else count
    fetched = [
        (tiles, rows // PB, wide, PB, SIG),
        (tiles, rows // PB, wide, PB, SIG),
        (tiles, rows, cols, SIG),
    ]
    handed = fetched if role == "first" else []
    kept = fetched if role == "" else []
    return pl.pallas_call(
        lambda *refs: fit_kernel(chunk, raws, role, *refs),
        in_specs=[WHOLE] * 3 + [HBM] + [operand] * 3 + [HBM],
        out_specs=[HBM, WHOLE] + [WHOLE] * len(handed),
        out_shape=[
            jax.ShapeDtypeStruct(fitted.shape, jnp.bfloat16),
            jax.ShapeDtypeStruct(acc.shape, jnp.float32),
        ] + [jax.ShapeDtypeStruct(shape, jnp.bfloat16) for shape in handed],
        scratch_shapes=[pltpu.VMEM(shape, jnp.bfloat16) for shape in kept] + [
            pltpu.VMEM(far.shape, jnp.bfloat16),
            pltpu.VMEM((tiles, rows, RAW_STEP if raws else 16, SIG), jnp.bfloat16),
            pltpu.VMEM((tiles, rows, count, SIG), jnp.bfloat16),
            pltpu.VMEM(((rows + 1) * (count + 1) + 8, SIG), jnp.float32),
            pltpu.SemaphoreType.DMA((tiles,)),
            pltpu.SemaphoreType.DMA((5, tiles)),
        ],
        input_output_aliases={len(args) - 1: 0},
        compiler_params=params(FIT_MIB),
        cost_estimate=cost(FIT_COST),
    )(*args)


def sum_pa(value):
    size = lax.axis_size("pa")

    def moved(value, stride, count, k):
        span = stride * count
        pairs = [
            (i, (i // span) * span + ((i // stride + k) % count) * stride + i % stride)
            for i in range(size)
        ]
        return lax.ppermute(value, "pa", pairs)

    value = value + moved(value, 1, 2, 1)
    for stride in (2, 8):
        parts = [moved(value, stride, 4, k) for k in (1, 2, 3)]
        value = (value + parts[1]) + (parts[0] + parts[2])
    return value


def after(value, *earlier):
    return lax.optimization_barrier((value,) + earlier)[0]


def on_device(three_center, center_mask, density, density_mask, metric_band):
    rows, cols, width = three_center.shape
    size = lax.axis_size("pa")
    near_pairs = [(i, i ^ 1) for i in range(size)]
    far_pairs = [(i, i + 1 if i % 2 else i - 1) for i in range(1, size - 1)]

    def to_far(value, *earlier):
        return lax.ppermute(after(value, *earlier), "pa", far_pairs)

    raw = raw_slice(three_center, center_mask)
    raw_far = to_far(raw)
    mask = jnp.repeat(center_mask, BS, axis=2).astype(jnp.float32)
    block_mask = jnp.repeat(jnp.repeat(density_mask, BS, axis=0), BS, axis=1)
    local = after(density * block_mask.astype(jnp.bfloat16), raw)
    count = lax.axis_size("mu")
    parts = [local] + [
        lax.ppermute(local, "mu", [((i + k) % count, i) for i in range(count)])
        for k in range(1, count)
    ]
    left, middle, right = jnp.split(metric_band, 3, axis=1)
    metric = jnp.where(
        lax.axis_index("pa") % 2 == 0,
        metric_band,
        jnp.concatenate([right, middle, left], axis=1),
    )

    def to_near(value):
        return lax.ppermute(value, "pa", near_pairs)

    dens, low, *rest = half_call(three_center, mask, parts)
    own_raw, chunks = rest[:2], rest[2:]
    far = [to_far(chunks[0])]
    near_raw = [to_near(piece) for piece in own_raw]
    near_low = to_near(low)
    fitted, acc = raw_call(raw_far, own_raw, near_raw, dens, metric, three_center, cols)
    far += [to_far(chunks[1], acc), to_far(chunks[2], acc)]
    handed = (low, near_low, three_center)
    for c, chunk in enumerate(CHUNKS):
        role = {len(CHUNKS) - 2: "first", len(CHUNKS) - 1: "second"}.get(c, "")
        fitted, acc, *rest = fit_call(
            chunk, role, far[c], *handed[:2], metric, handed[2], mask, acc, fitted
        )
        handed = tuple(rest) or handed
        if len(far) < len(CHUNKS):
            far.append(to_far(chunks[len(far)], acc))
    scale = 1.0 / math.sqrt(rows * size * width)
    return (fitted, sum_pa(acc) * scale)


def solution(mesh):
    placed = (P("pa", "mu", None), P("pa", "mu", None), P("mu", None), P("mu", None), P("pa", None))
    return jax.shard_map(
        on_device,
        mesh=mesh,
        in_specs=placed,
        out_specs=(P("pa", "mu", None), P("mu", None)),
        check_vma=False,
    )
```

```python
import math

import jax
import jax.numpy as jnp
from jax import lax
from jax.experimental import pallas as pl
from jax.experimental.pallas import tpu as pltpu
from jax.sharding import PartitionSpec as P

BS = 64
SIG = 128
PB = 16
QB = 16
MIB = 2**20

RAW_MU = 32
RAW_STEP = 32
LOW = (0, 4, 0, 32)
RAW_HALVES = ((0, 2, 32, 32), (256, 2, 32, 32))
CHUNKS = ((0, 2, 0, 32), (256, 1, 0, 32), (384, 1, 0, 16), (384, 1, 16, 16))
PIECES = (LOW,) + RAW_HALVES + CHUNKS
HALF_MIB = 56
HALF_COST = 1
FIT_MIB = 40
RAW_MIB = 32
FIT_COST = 0.3
HBM = pl.BlockSpec(memory_space=pltpu.HBM)
WHOLE = pl.BlockSpec(memory_space=pltpu.VMEM)


def cost(us):
    return pl.CostEstimate(
        flops=int(us * 4e9), bytes_accessed=int(us * 12e6), transcendentals=0
    )


def params(mib):
    return pltpu.CompilerParams(vmem_limit_bytes=mib * MIB)


def half_rows(x, dens, scratch, cols):
    flat = jnp.dot(x.reshape(PB * cols, x.shape[2]), dens, preferred_element_type=jnp.float32)
    pitch = cols + 1
    for t in range(scratch.shape[0]):
        for p in range(PB):
            scratch[t, p * pitch:p * pitch + cols] = flat[
                p * cols:(p + 1) * cols, t * SIG:(t + 1) * SIG
            ]


def turned(scratch, t, m, cols):
    return scratch[t, pl.ds(m, PB, stride=cols + 1), :].astype(jnp.bfloat16)


def half_kernel(mask_ref, *refs):
    parts, tc_hbm = refs[:4], refs[4]
    dens_ref, outs = refs[5], refs[6:-5]
    tc_buf, staged, scratch, in_sem, out_sem = refs[-5:]
    rows, cols, width = tc_buf.shape
    blocks = rows // PB

    def fetch(b):
        rows_b = pl.ds(b * PB, PB)
        return pltpu.make_async_copy(tc_hbm.at[rows_b], tc_buf.at[rows_b], in_sem.at[b])

    for b in range(blocks):
        fetch(b).start()
    me = lax.axis_index("mu")
    depth = parts[0].shape[0]
    for k, part in enumerate(parts):
        at = lax.rem(me + k, len(parts)) * depth
        dens_ref[pl.ds(pl.multiple_of(at, depth), depth), :] = part[...]

    def step(b, carry):
        fetch(b).wait()
        x = tc_buf[pl.ds(b * PB, PB)] * mask_ref[(b * PB) // BS].astype(jnp.bfloat16)
        half_rows(x, dens_ref[...], scratch, cols)
        for t in range(width // SIG):
            for m in range(cols):
                staged[t, b, m] = turned(scratch, t, m, cols)
        for k, (s, tiles, mu0, count) in enumerate(PIECES):
            part = staged.at[pl.ds(s // SIG, tiles), b, pl.ds(mu0, count)]
            pltpu.make_async_copy(part, outs[k].at[:, b], out_sem.at[k]).start()
        return carry

    lax.fori_loop(0, blocks, step, 0)
    for k, (s, tiles, mu0, count) in enumerate(PIECES):
        part = staged.at[pl.ds(s // SIG, tiles), :, pl.ds(mu0, count)]
        pltpu.make_async_copy(part, outs[k], out_sem.at[k]).wait()


def half_call(tc, mask, parts):
    rows, cols, width = tc.shape
    whole = (width // SIG, rows // PB, cols, PB, SIG)
    shapes = [(width, width)] + [(t, rows // PB, n, PB, SIG) for _, t, _, n in PIECES]
    return pl.pallas_call(
        half_kernel,
        in_specs=[WHOLE] * (1 + len(parts)) + [HBM],
        out_specs=[WHOLE] + [HBM] * len(PIECES),
        out_shape=[jax.ShapeDtypeStruct(shape, jnp.bfloat16) for shape in shapes],
        scratch_shapes=[
            pltpu.VMEM(tc.shape, jnp.bfloat16),
            pltpu.VMEM(whole, jnp.bfloat16),
            pltpu.VMEM((width // SIG, (PB + 1) * (cols + 1) + 8, SIG), jnp.float32),
            pltpu.SemaphoreType.DMA((rows // PB,)),
            pltpu.SemaphoreType.DMA((len(PIECES),)),
        ],
        compiler_params=params(HALF_MIB),
        cost_estimate=cost(HALF_COST),
    )(mask, *parts, tc)


def raw_kernel_send(mask_ref, tc, out, bufs, in_sem, out_sem):
    rows, count, width = bufs.shape
    step = rows // in_sem.shape[0]

    def fetch(b):
        part = pl.ds(b * step, step)
        source = tc.at[part, pl.ds(RAW_MU, RAW_STEP)]
        return pltpu.make_async_copy(source, bufs.at[part], in_sem.at[b])

    def put(b):
        part = pl.ds(b * step, step)
        return pltpu.make_async_copy(bufs.at[part], out.at[part], out_sem.at[b])

    pieces = rows // step
    for b in range(pieces):
        fetch(b).start()
    block = lax.broadcasted_iota(jnp.int32, (1, width), 1) // BS
    masks = []
    for p in range(mask_ref.shape[0]):
        lanes = jnp.zeros((1, width), jnp.float32)
        for k in range(mask_ref.shape[2]):
            lanes = jnp.where(block == k, mask_ref[p, 0, k].astype(jnp.float32), lanes)
        masks.append(lanes.astype(jnp.bfloat16))
    for b in range(pieces):
        fetch(b).wait()
        mask = masks[(b * step) // BS]

        def scale(i, carry, mask=mask, b=b):
            row = b * step + i
            bufs[row] = bufs[row] * mask
            return carry

        lax.fori_loop(0, step, scale, 0, unroll=4)
        put(b).start()
    for b in range(pieces):
        put(b).wait()


def raw_slice(tc, center_mask):
    rows, _, width = tc.shape
    pieces = 4
    return pl.pallas_call(
        raw_kernel_send,
        in_specs=[pl.BlockSpec(memory_space=pltpu.SMEM), HBM],
        out_specs=HBM,
        out_shape=jax.ShapeDtypeStruct((rows, RAW_STEP, width), tc.dtype),
        scratch_shapes=[
            pltpu.VMEM((rows, RAW_STEP, width), tc.dtype),
            pltpu.SemaphoreType.DMA((pieces,)),
            pltpu.SemaphoreType.DMA((pieces,)),
        ],
        compiler_params=params(HALF_MIB),
        cost_estimate=cost(FIT_COST),
    )(center_mask, tc)


def fit_tile(pieces, metric_ref, scratch, pitch, count):
    metric = metric_ref[...]
    rows = metric.shape[0]

    def fit(pair, carry):
        columns = [jnp.concatenate(pieces(m), axis=0) for m in (2 * pair, 2 * pair + 1)]
        y = jnp.dot(metric, jnp.concatenate(columns, axis=1), preferred_element_type=jnp.float32)
        scratch[pl.ds(2 * pair, rows, stride=pitch), :] = y[:, :SIG]
        scratch[pl.ds(2 * pair + 1, rows, stride=pitch), :] = y[:, SIG:]
        return carry

    lax.fori_loop(0, count // 2, fit, 0, unroll=8)


def raw_kernel(metric_ref, dens_ref, raw, *refs):
    own, near, refs = refs[:2], refs[2:4], refs[4:]
    fitted, zero_ref, raw_buf, far_buf, own_buf, near_buf, staged, half_scratch, scratch = refs[:9]
    raw_sem, in_sem, out_sem = refs[9:]
    tiles, rows, count, _ = staged.shape
    pitch = count + 1
    blocks = rows // PB

    def fetch_raw(b):
        part = pl.ds(b * PB, PB)
        return pltpu.make_async_copy(raw.at[part], raw_buf.at[part], raw_sem.at[b])

    def fetch(t):
        k, at = t // 2, t % 2
        return [
            pltpu.make_async_copy(own[k].at[at], own_buf.at[t], in_sem.at[0, t]),
            pltpu.make_async_copy(near[k].at[at], near_buf.at[t], in_sem.at[1, t]),
        ]

    def put(t):
        lanes = pl.ds(t * SIG, SIG)
        return pltpu.make_async_copy(
            staged.at[t], fitted.at[:, pl.ds(RAW_MU, count), lanes], out_sem.at[t]
        )

    for b in range(blocks):
        fetch_raw(b).start()
    for t in range(tiles):
        for copy in fetch(t):
            copy.start()
    zero_ref[...] = jnp.zeros(zero_ref.shape, jnp.float32)

    def step(b, carry):
        fetch_raw(b).wait()
        half_rows(raw_buf[pl.ds(b * PB, PB)], dens_ref[...], half_scratch, count)
        for t in range(tiles):
            for m in range(count):
                far_buf[t, b, m] = turned(half_scratch, t, m, count)
        return carry

    lax.fori_loop(0, blocks, step, 0)
    for t in range(tiles):
        for copy in fetch(t):
            copy.wait()

        def pieces(m, t=t):
            return [buf[t, :, m].reshape(rows, SIG) for buf in (far_buf, own_buf, near_buf)]

        fit_tile(pieces, metric_ref, scratch, pitch, count)

        def store(block, inner, t=t):
            for q in range(QB):
                row = block * QB + q
                staged[t, row] = scratch[pl.ds(row * pitch, count), :].astype(jnp.bfloat16)
            return inner

        lax.fori_loop(0, rows // QB, store, 0)
        put(t).start()
    for t in range(tiles):
        put(t).wait()


def raw_call(raw_far, own, near, dens, metric, tc, cols):
    rows, count, width = raw_far.shape
    tiles = width // SIG
    buf = pltpu.VMEM((tiles, rows // PB, count, PB, SIG), jnp.bfloat16)
    return pl.pallas_call(
        raw_kernel,
        in_specs=[WHOLE, WHOLE] + [HBM] * 5,
        out_specs=[HBM, WHOLE],
        out_shape=[
            jax.ShapeDtypeStruct(tc.shape, jnp.bfloat16),
            jax.ShapeDtypeStruct((cols, cols), jnp.float32),
        ],
        scratch_shapes=[
            pltpu.VMEM(raw_far.shape, jnp.bfloat16),
            buf,
            buf,
            buf,
            pltpu.VMEM((tiles, rows, count, SIG), jnp.bfloat16),
            pltpu.VMEM((tiles, (PB + 1) * (count + 1) + 8, SIG), jnp.float32),
            pltpu.VMEM(((rows + 1) * (count + 1) + 8, SIG), jnp.float32),
            pltpu.SemaphoreType.DMA((rows // PB,)),
            pltpu.SemaphoreType.DMA((2, tiles)),
            pltpu.SemaphoreType.DMA((tiles,)),
        ],
        compiler_params=params(RAW_MIB),
        cost_estimate=cost(FIT_COST),
    )(metric, dens, raw_far, *own, *near)


def fit_kernel(chunk, raws, role, metric_ref, mask_ref, acc_ref, far, *refs):
    s, tiles, mu0, count = chunk
    (own, near, tc, _, fitted, exch_ref), refs = refs[:6], refs[6:]
    if role == "second":
        own_buf, near_buf, tc_buf = own, near, tc
        base = mu0
        far_buf, raw_buf, staged, scratch, out_sem, in_sem = refs
    else:
        own_buf, near_buf, tc_buf, far_buf, raw_buf, staged, scratch, out_sem, in_sem = refs
        base = 0
    rows = metric_ref.shape[0]
    pitch = count + 1
    wide = own_buf.shape[2]

    def fetch(t):
        part = pl.ds(mu0, wide)
        lanes = pl.ds(s + t * SIG, SIG)
        tile = s // SIG + t
        copies = [pltpu.make_async_copy(far.at[t], far_buf.at[t], in_sem.at[0, t])]
        if raws:
            source = fitted.at[:, pl.ds(RAW_MU, RAW_STEP), lanes]
            copies.append(pltpu.make_async_copy(source, raw_buf.at[t], in_sem.at[4, t]))
        if role == "second":
            return copies
        return copies + [
            pltpu.make_async_copy(own.at[tile, :, part], own_buf.at[t], in_sem.at[1, t]),
            pltpu.make_async_copy(near.at[tile, :, part], near_buf.at[t], in_sem.at[2, t]),
            pltpu.make_async_copy(tc.at[:, :, lanes], tc_buf.at[t], in_sem.at[3, t]),
        ]

    def put(t):
        lanes = pl.ds(s + t * SIG, SIG)
        return pltpu.make_async_copy(
            staged.at[t], fitted.at[:, pl.ds(mu0, count), lanes], out_sem.at[t]
        )

    for t in range(tiles):
        for copy in fetch(t):
            copy.start()
    exch_ref[...] = acc_ref[...]
    for t in range(tiles):
        for copy in fetch(t):
            copy.wait()

        def pieces(m, t=t):
            bufs = (far_buf[t, :, m], own_buf[t, :, base + m], near_buf[t, :, base + m])
            return [piece.reshape(rows, SIG) for piece in bufs]

        fit_tile(pieces, metric_ref, scratch, pitch, count)
        def contract(block, total, t=t):
            first = pl.multiple_of(block * QB, QB)
            lanes = slice(s + t * SIG, s + (t + 1) * SIG)
            mask = mask_ref[(block * QB) // BS, :, lanes].astype(jnp.bfloat16)
            left = []
            for q in range(QB):
                f = scratch[pl.ds((first + q) * pitch, count), :].astype(jnp.bfloat16)
                staged[t, first + q] = f
                if raws:
                    f = jnp.concatenate([f, raw_buf[t, first + q]], axis=0)
                left.append(f * mask)
            right = [tc_buf[t, first + q] for q in range(QB)]
            return total + lax.dot_general(
                jnp.concatenate(left, axis=1),
                jnp.concatenate(right, axis=1),
                (((1,), (1,)), ((), ())),
                preferred_element_type=jnp.float32,
            )

        lines = count + raws * RAW_STEP
        total = lax.fori_loop(
            0, rows // QB, contract, jnp.zeros((lines, acc_ref.shape[1]), jnp.float32), unroll=2
        )
        put(t).start()
        exch_ref[mu0:mu0 + count, :] += total[:count]
        if raws:
            exch_ref[RAW_MU:, :] += total[count:]
    for t in range(tiles):
        put(t).wait()


def fit_call(chunk, role, far, own, near, metric, tc, mask, acc, fitted):
    _, tiles, _, count = chunk
    rows, cols = metric.shape[0], acc.shape[1]
    raws = 0 if role == "second" else 1
    args = [metric, mask, acc, far, own, near, tc, fitted]
    operand = WHOLE if role == "second" else HBM
    wide = 2 * count if role == "first" else count
    fetched = [
        (tiles, rows // PB, wide, PB, SIG),
        (tiles, rows // PB, wide, PB, SIG),
        (tiles, rows, cols, SIG),
    ]
    handed = fetched if role == "first" else []
    kept = fetched if role == "" else []
    return pl.pallas_call(
        lambda *refs: fit_kernel(chunk, raws, role, *refs),
        in_specs=[WHOLE] * 3 + [HBM] + [operand] * 3 + [HBM],
        out_specs=[HBM, WHOLE] + [WHOLE] * len(handed),
        out_shape=[
            jax.ShapeDtypeStruct(fitted.shape, jnp.bfloat16),
            jax.ShapeDtypeStruct(acc.shape, jnp.float32),
        ] + [jax.ShapeDtypeStruct(shape, jnp.bfloat16) for shape in handed],
        scratch_shapes=[pltpu.VMEM(shape, jnp.bfloat16) for shape in kept] + [
            pltpu.VMEM(far.shape, jnp.bfloat16),
            pltpu.VMEM((tiles, rows, RAW_STEP if raws else 16, SIG), jnp.bfloat16),
            pltpu.VMEM((tiles, rows, count, SIG), jnp.bfloat16),
            pltpu.VMEM(((rows + 1) * (count + 1) + 8, SIG), jnp.float32),
            pltpu.SemaphoreType.DMA((tiles,)),
            pltpu.SemaphoreType.DMA((5, tiles)),
        ],
        input_output_aliases={len(args) - 1: 0},
        compiler_params=params(FIT_MIB),
        cost_estimate=cost(FIT_COST),
    )(*args)


def sum_pa(value):
    size = lax.axis_size("pa")

    def swapped(value, mask):
        return lax.ppermute(value, "pa", [(i, i ^ mask) for i in range(size)])

    for first, second in ((1, 2), (6, 8)):
        a, b, both = (swapped(value, mask) for mask in (first, second, first ^ second))
        value = (value + a) + (b + both)
    return value + swapped(value, 24)


def after(value, *earlier):
    return lax.optimization_barrier((value,) + earlier)[0]


def on_device(three_center, center_mask, density, density_mask, metric_band):
    rows, cols, width = three_center.shape
    size = lax.axis_size("pa")
    near_pairs = [(i, i ^ 1) for i in range(size)]
    far_pairs = [(i, i + 1 if i % 2 else i - 1) for i in range(1, size - 1)]

    def to_far(value, *earlier):
        return lax.ppermute(after(value, *earlier), "pa", far_pairs)

    raw = raw_slice(three_center, center_mask)
    raw_far = to_far(raw)
    mask = jnp.repeat(center_mask, BS, axis=2).astype(jnp.float32)
    block_mask = jnp.repeat(jnp.repeat(density_mask, BS, axis=0), BS, axis=1)
    local = after(density * block_mask.astype(jnp.bfloat16), raw)
    count = lax.axis_size("mu")
    parts = [local] + [
        lax.ppermute(local, "mu", [((i + k) % count, i) for i in range(count)])
        for k in range(1, count)
    ]
    left, middle, right = jnp.split(metric_band, 3, axis=1)
    metric = jnp.where(
        lax.axis_index("pa") % 2 == 0,
        metric_band,
        jnp.concatenate([right, middle, left], axis=1),
    )

    def to_near(value):
        return lax.ppermute(value, "pa", near_pairs)

    dens, low, *rest = half_call(three_center, mask, parts)
    own_raw, chunks = rest[:2], rest[2:]
    far = [to_far(chunks[0])]
    near_raw = [to_near(piece) for piece in own_raw]
    near_low = to_near(low)
    fitted, acc = raw_call(raw_far, own_raw, near_raw, dens, metric, three_center, cols)
    far += [to_far(chunks[1], acc), to_far(chunks[2], acc)]
    handed = (low, near_low, three_center)
    for c, chunk in enumerate(CHUNKS):
        role = {len(CHUNKS) - 2: "first", len(CHUNKS) - 1: "second"}.get(c, "")
        fitted, acc, *rest = fit_call(
            chunk, role, far[c], *handed[:2], metric, handed[2], mask, acc, fitted
        )
        handed = tuple(rest) or handed
        if len(far) < len(CHUNKS):
            far.append(to_far(chunks[len(far)], acc))
    scale = 1.0 / math.sqrt(rows * size * width)
    return (fitted, sum_pa(acc) * scale)


def solution(mesh):
    placed = (P("pa", "mu", None), P("pa", "mu", None), P("mu", None), P("mu", None), P("pa", None))
    return jax.shard_map(
        on_device,
        mesh=mesh,
        in_specs=placed,
        out_specs=(P("pa", "mu", None), P("mu", None)),
        check_vma=False,
    )
```
